128 devices in a mesh: dp: 128 (over y, z, x, core).
Axes of the slice: x: 4, y: 4, z: 4, core: 2. Of those that a mesh axis runs over, the one named last changes fastest.
Arguments:
- text_states: bfloat16 [512, 16, 768], P('dp'), may hold values from -6 to 6
- image_states: bfloat16 [512, 197, 768], P('dp'), may hold values from -6 to 6
- cot_positive: bfloat16 [512, 16, 768], P('dp'), may hold values from -6 to 6
- cot_neg_image: bfloat16 [512, 16, 768], P('dp'), may hold values from -6 to 6
- cot_neg_text: bfloat16 [512, 16, 768], P('dp'), may hold values from -6 to 6
- w_query: bfloat16 [768, 768], replicated, may hold values from -0.57735027 to 0.57735027
- w_key: bfloat16 [768, 768], replicated, may hold values from -0.57735027 to 0.57735027
- w_value: bfloat16 [768, 768], replicated, may hold values from -0.21875 to 0.21875
- w_out: bfloat16 [768, 768], replicated, may hold values from -0.21875 to 0.21875
- ln_gain: float32 [768], replicated, may hold values from 0.5 to 1.5
- neg_image: int32 [512], P('dp'), may hold values from 0 to 511, as said below
- neg_text: int32 [512], P('dp'), may hold values from 0 to 511, as said below
- text_feat: bfloat16 [512, 256], P('dp'), may hold values from -8 to 8
- image_feat: bfloat16 [512, 256], P('dp'), may hold values from -8 to 8
Outputs:
- d_text: bfloat16 [512, 16, 768], P('dp')
- d_image: bfloat16 [512, 197, 768], P('dp')
- d_text_feat: float32 [512, 256], P('dp')
- d_image_feat: float32 [512, 256], P('dp')
The draws below stay inside these ranges and needn't reach their ends.
Inputs may be any that keep to these rules, and one draw needn't show every extreme that they name: `neg_image`: every hard-negative image lies on another device than its text. The 4 texts of one device name images of 4 different devices. The images of one device are named by at most 8 texts in all, and those of some device by exactly 8. `neg_text`: every hard-negative text lies on another device than its image. The 4 images of one device name texts of 4 different devices.
All inputs are finite; a program needn't handle non-finite values.
Results may differ from the reference program's by a relative error of at most 0.034.
Values may be sent and summed in bfloat16 or wider, within the bound.
No kernel may reach another device: no remote copies, remote signals or barrier semaphores. Data moves between devices by JAX's collectives and lax.ppermute only.
A program may use at most 128 MiB of HBM per device.

```python
import math
import jax
import jax.numpy as jnp
from jax import lax

D = 768
H = 12
E = 256
LT = 16
LI = 197
P_DEV = 4
TOTAL = 512


def spread_owners(key, dev_count, count):
    split_keys = jax.random.split(key, 2)
    offsets = jax.random.permutation(split_keys[0], dev_count - 1).astype(jnp.int32)[:count] + 1
    relabel = jax.random.permutation(split_keys[1], dev_count).astype(jnp.int32)
    position = jnp.argsort(relabel, stable=True).astype(jnp.int32)
    return relabel[(position[:, None] + offsets[None, :]) % dev_count]


def projection_draw(key):
    split_keys = jax.random.split(key, 1)
    matrix = jax.random.normal(split_keys[0], (D, D), jnp.float32) / math.sqrt(D)
    bound_value = 16.0 / math.sqrt(D)
    return jnp.clip(matrix, -bound_value, bound_value).astype(jnp.bfloat16)


def draw_w_query(key, part):
    key = jax.random.fold_in(key, 31)
    return projection_draw(key)


def draw_w_key(key, part):
    key = jax.random.fold_in(key, 33)
    return projection_draw(key)


def draw_neg_image(key, part):
    key = jax.random.fold_in(key, 11)
    dev_count = TOTAL // P_DEV
    extra = min(2 * P_DEV, dev_count - 1) - P_DEV
    split_keys = jax.random.split(key, 6)
    devices = jnp.arange(dev_count, dtype=jnp.int32)
    owners = spread_owners(split_keys[0], dev_count, P_DEV)
    hottest = jax.random.randint(split_keys[1], (), 0, dev_count)
    sends_hot = jnp.any(owners == hottest, axis=1)
    eligible = jnp.logical_and(jnp.logical_not(sends_hot), devices != hottest)
    ranking = jax.random.permutation(split_keys[2], dev_count).astype(jnp.int32)
    scoring = jnp.where(eligible, ranking, ranking + dev_count)
    chosen = jnp.argsort(scoring, stable=True)[:extra].astype(jnp.int32)
    picked = jnp.any(devices[:, None] == chosen[None, :], axis=1)
    which_text = jax.random.randint(split_keys[3], (dev_count,), 0, P_DEV)
    redirect = jnp.logical_and(picked[:, None], jnp.arange(P_DEV)[None, :] == which_text[:, None])
    owners = jnp.where(redirect, hottest, owners)
    local_ids = jax.random.randint(split_keys[4], (dev_count, P_DEV), 0, P_DEV)
    hot_local = jax.random.randint(split_keys[5], (), 0, P_DEV)
    local_ids = jnp.where(redirect, hot_local, local_ids)
    return (owners * P_DEV + local_ids).reshape(-1).astype(jnp.int32)


def draw_neg_text(key, part):
    key = jax.random.fold_in(key, 13)
    dev_count = TOTAL // P_DEV
    split_keys = jax.random.split(key, 2)
    owners = spread_owners(split_keys[0], dev_count, P_DEV)
    local_ids = jax.random.randint(split_keys[1], (dev_count, P_DEV), 0, P_DEV)
    return (owners * P_DEV + local_ids).reshape(-1).astype(jnp.int32)


def draw_image_feat(key, part):
    key = jax.random.fold_in(key, 21)
    own_part = jax.random.normal(key, (TOTAL, E), jnp.float32)
    mixed = own_part
    return jnp.clip(mixed, -8.0, 8.0).astype(jnp.bfloat16)


def draw_text_feat(key, part):
    key = jax.random.fold_in(key, 23)
    split_keys = jax.random.split(key, 1)
    own_part = jax.random.normal(split_keys[0], (TOTAL, E), jnp.float32)
    mixed = own_part
    return jnp.clip(mixed, -8.0, 8.0).astype(jnp.bfloat16)


def levels(rng, shape, cuts, low, top_value):
    def one(dim, shards_of):
        steps = jax.random.uniform(jax.random.fold_in(jax.random.fold_in(rng, 6), dim), (shards_of,), jnp.float32, low / len(cuts), top_value / len(cuts))
        return jnp.repeat(jnp.exp(steps), shape[dim] // shards_of).reshape((-1,) + (1,) * (len(shape) - dim - 1))

    loudness = one(*cuts[0])
    for cut in cuts[1:]:
        loudness = loudness * one(*cut)
    return loudness


def normal_values(own_key, shape, deviation, limit, cuts=(), kind=jnp.bfloat16):
    gain = levels(own_key, shape, cuts, -0.22, 0.18) if cuts else 1.0
    entries = jax.random.normal(own_key, shape, jnp.float32) * deviation * gain
    return jnp.minimum(jnp.maximum(entries, -limit), limit).astype(kind)


def setup_inputs(seed: int = 0) -> dict:
    key_of = jax.random.split(jax.random.key(seed), 15)
    return {
        "text_states": normal_values(key_of[0], (TOTAL, LT, D), 1.0, 6.0, ((0, 128),)),
        "image_states": normal_values(key_of[1], (TOTAL, LI, D), 1.0, 6.0, ((0, 128),)),
        "cot_positive": normal_values(key_of[2], (TOTAL, LT, D), 1.0, 6.0, ((0, 128),)),
        "cot_neg_image": normal_values(key_of[3], (TOTAL, LT, D), 1.0, 6.0, ((0, 128),)),
        "cot_neg_text": normal_values(key_of[4], (TOTAL, LT, D), 1.0, 6.0, ((0, 128),)),
        "w_query": draw_w_query(jax.random.fold_in(key_of[14], 71), 0),
        "w_key": draw_w_key(jax.random.fold_in(key_of[14], 71), 0),
        "w_value": normal_values(key_of[7], (D, D), D ** -0.5, 0.21875),
        "w_out": normal_values(key_of[8], (D, D), D ** -0.5, 0.21875),
        "ln_gain": jnp.clip(1.0 + 0.1 * jax.random.normal(key_of[9], (D,), jnp.float32), 0.5, 1.5),
        "neg_image": draw_neg_image(jax.random.fold_in(key_of[14], 71), 0),
        "neg_text": draw_neg_text(jax.random.fold_in(key_of[14], 71), 0),
        "text_feat": draw_text_feat(jax.random.fold_in(key_of[14], 71), 0),
        "image_feat": draw_image_feat(jax.random.fold_in(key_of[14], 71), 0),
    }


norm_eps = 1e-06

def layer_back(texts, cotangent, key_rows, value_rows, w_query, w_out, ln_gain):
    batch_size, text_len, model_dim = texts.shape
    head_dim = model_dim // H
    inv_root = 1.0 / math.sqrt(head_dim)
    flat_text = texts.reshape(batch_size * text_len, model_dim)
    queries = jnp.dot(flat_text, w_query, preferred_element_type=jnp.float32).astype(jnp.bfloat16)
    query_heads = queries.reshape(batch_size, text_len, H, head_dim)
    key_heads = key_rows.reshape(batch_size, -1, H, head_dim)
    value_heads = value_rows.reshape(batch_size, -1, H, head_dim)
    scores = jnp.einsum('bqhe,bkhe->bhqk', query_heads.astype(jnp.float32), key_heads.astype(jnp.float32)) * inv_root
    weights = jnp.exp(scores - lax.optimization_barrier(jnp.max(scores, axis=-1, keepdims=True)))
    weights = weights / lax.optimization_barrier(jnp.sum(weights, axis=-1, keepdims=True))
    probs_half = weights.astype(jnp.bfloat16)
    context = jnp.einsum('bhqk,bkhe->bqhe', probs_half.astype(jnp.float32), value_heads.astype(jnp.float32))
    context = context.astype(jnp.bfloat16).reshape(batch_size * text_len, model_dim)
    attended = jnp.dot(context, w_out, preferred_element_type=jnp.float32)
    summed = attended + flat_text.astype(jnp.float32)
    centred = summed - lax.optimization_barrier(jnp.mean(summed, axis=-1, keepdims=True))
    inv_sigma = lax.rsqrt(lax.optimization_barrier(jnp.mean(centred * centred, axis=-1, keepdims=True)) + norm_eps)
    normed = centred * inv_sigma
    grad_norm = cotangent.reshape(-1, model_dim).astype(jnp.float32) * ln_gain
    d_summed = inv_sigma * (grad_norm - lax.optimization_barrier(jnp.mean(grad_norm, axis=-1, keepdims=True)) - normed * lax.optimization_barrier(jnp.mean(grad_norm * normed, axis=-1, keepdims=True)))
    d_context = jnp.dot(d_summed.astype(jnp.bfloat16), w_out.T, preferred_element_type=jnp.float32)
    d_context = d_context.astype(jnp.bfloat16).reshape(batch_size, text_len, H, head_dim)
    d_probs = jnp.einsum('bqhe,bkhe->bhqk', d_context.astype(jnp.float32), value_heads.astype(jnp.float32))
    d_values = jnp.einsum('bhqk,bqhe->bkhe', probs_half.astype(jnp.float32), d_context.astype(jnp.float32))
    d_values = d_values.reshape(batch_size, -1, model_dim)
    d_scores = weights * (d_probs - lax.optimization_barrier(jnp.sum(weights * d_probs, axis=-1, keepdims=True))) * inv_root
    d_scores = d_scores.astype(jnp.bfloat16)
    d_queries = jnp.einsum('bhqk,bkhe->bqhe', d_scores.astype(jnp.float32), key_heads.astype(jnp.float32))
    d_queries = d_queries.astype(jnp.bfloat16).reshape(-1, model_dim)
    d_keys = jnp.einsum('bhqk,bqhe->bkhe', d_scores.astype(jnp.float32), query_heads.astype(jnp.float32))
    d_keys = d_keys.reshape(batch_size, -1, model_dim)
    d_texts = d_summed + jnp.dot(d_queries, w_query.T, preferred_element_type=jnp.float32)
    return (d_texts.reshape(batch_size, text_len, model_dim), d_keys, d_values)

def reference(text_states, image_states, cot_positive, cot_neg_image, cot_neg_text, w_query, w_key, w_value, w_out, ln_gain, neg_image, neg_text, text_feat, image_feat):
    total_pairs = text_states.shape[0]
    flat_images = image_states.reshape(total_pairs * LI, D)
    image_keys = jnp.dot(flat_images, w_key, preferred_element_type=jnp.float32).astype(jnp.bfloat16)
    image_keys = image_keys.reshape(total_pairs, LI, D)
    image_values = jnp.dot(flat_images, w_value, preferred_element_type=jnp.float32).astype(jnp.bfloat16)
    image_values = image_values.reshape(total_pairs, LI, D)
    pair_ids = jnp.arange(total_pairs, dtype=jnp.int32)
    all_texts = jnp.concatenate([text_states, jnp.take(text_states, neg_text.astype(jnp.int32), axis=0), text_states], axis=0)
    all_cots = jnp.concatenate([cot_positive, cot_neg_text, cot_neg_image], axis=0)
    all_targets = jnp.concatenate([pair_ids, pair_ids, neg_image.astype(jnp.int32)]).astype(jnp.int32)
    block_len = P_DEV
    block_count = 3 * total_pairs // block_len

    def visit(carry, index):
        key_acc, value_acc = carry
        start = (index * block_len).astype(jnp.int32)
        texts_blk = lax.dynamic_slice_in_dim(all_texts, start, block_len, 0)
        cots_blk = lax.dynamic_slice_in_dim(all_cots, start, block_len, 0)
        target_blk = lax.dynamic_slice_in_dim(all_targets, start, block_len, 0)
        d_texts_blk, d_keys_blk, d_values_blk = layer_back(texts_blk, cots_blk, jnp.take(image_keys, target_blk, axis=0), jnp.take(image_values, target_blk, axis=0), w_query, w_out, ln_gain)
        return ((key_acc.at[target_blk].add(d_keys_blk), value_acc.at[target_blk].add(d_values_blk)), d_texts_blk)
    zero_acc = jnp.zeros((total_pairs, LI, D), jnp.float32)
    (key_acc, value_acc), d_texts = lax.scan(visit, (zero_acc, zero_acc), jnp.arange(block_count, dtype=jnp.int32))
    d_texts = d_texts.reshape(3 * total_pairs, LT, D)
    d_keys = key_acc.astype(jnp.bfloat16).reshape(-1, D)
    d_values = value_acc.astype(jnp.bfloat16).reshape(-1, D)
    d_image = jnp.dot(d_keys, w_key.T, preferred_element_type=jnp.float32) + jnp.dot(d_values, w_value.T, preferred_element_type=jnp.float32)
    d_image = d_image.astype(jnp.bfloat16).reshape(total_pairs, LI, D)
    pull_part = lax.optimization_barrier(d_texts[total_pairs:2 * total_pairs].astype(jnp.bfloat16)).astype(jnp.float32)
    push_part = lax.optimization_barrier(d_texts[2 * total_pairs:].astype(jnp.bfloat16)).astype(jnp.float32)
    pull_sum = jnp.zeros((total_pairs, LT, D), jnp.float32).at[neg_text.astype(jnp.int32)].add(pull_part)
    d_text = (d_texts[:total_pairs] + push_part + pull_sum).astype(jnp.bfloat16)
    sim_scale = 3.0 / math.sqrt(E)
    similar = jnp.dot(text_feat, image_feat.T, preferred_element_type=jnp.float32) * sim_scale
    row_peak = lax.optimization_barrier(jnp.max(similar, axis=1, keepdims=True))
    row_lse = row_peak + jnp.log(lax.optimization_barrier(jnp.sum(jnp.exp(similar - row_peak), axis=1, keepdims=True)))
    col_peak = lax.optimization_barrier(jnp.max(similar, axis=0, keepdims=True))
    col_lse = col_peak + jnp.log(lax.optimization_barrier(jnp.sum(jnp.exp(similar - col_peak), axis=0, keepdims=True)))
    identity_mat = jnp.eye(total_pairs, dtype=jnp.float32)
    d_similar = 0.5 * (jnp.exp(similar - row_lse) - identity_mat) + 0.5 * (jnp.exp(similar - col_lse) - identity_mat)
    d_text_feat = sim_scale * jnp.dot(d_similar, image_feat.astype(jnp.float32), precision=lax.Precision.HIGHEST)
    d_image_feat = sim_scale * jnp.dot(d_similar.T, text_feat.astype(jnp.float32), precision=lax.Precision.HIGHEST)
    return (d_text, d_image, d_text_feat, d_image_feat)
```

```python
import functools
import math

import jax
import jax.numpy as jnp
from jax import lax
from jax.experimental import pallas as pl
from jax.experimental.pallas import tpu as pltpu
from jax.sharding import PartitionSpec as P

D = 768
H = 12
E = 256
LT = 16
LI = 197
PAIRS = 4
DEVS = 128
TILE = 128
COLS = D // TILE
PIECES = COLS * LT
LIP = 256
LIR = 208
GROUP = 4
GROUPS = H // GROUP
GW = D // GROUPS
GR = GROUP * LT
INV_ROOT = 1.0 / math.sqrt(D // H)
NORM_EPS = 1e-06
SIM_SCALE = 3.0 / math.sqrt(E)
PUSH = 2 * PAIRS
BF = jnp.bfloat16
F32 = jnp.float32
VMEM_LIMIT = 48 * 1024 * 1024

NN = (((1,), (0,)), ((), ()))
NT = (((1,), (1,)), ((), ()))
TN = (((0,), (0,)), ((), ()))


def mm(a, b, dims=NN):
    return lax.dot_general(a, b, dims, preferred_element_type=F32)


def iota(shape, dim):
    return lax.broadcasted_iota(jnp.int32, shape, dim)


def one_hot(mask):
    return jnp.where(mask, 1.0, 0.0).astype(BF)


def pack_kernel(ni_ref, nt_ref, text_ref, cot_ref, tf_ref, if_ref, out_ref, common):
    tf = tf_ref[...].astype(F32)
    im = if_ref[...].astype(F32)
    common[0:4] = tf[:, :TILE]
    common[4:8] = im[:, :TILE]
    common[8:12] = tf[:, TILE:]
    common[12:16] = im[:, TILE:]
    row = iota((8, TILE), 0)
    lane = iota((8, TILE), 1)
    ids = jnp.full((8, TILE), -1, jnp.int32)
    for a in range(PAIRS):
        ni = ni_ref[a]
        nt = nt_ref[a]
        for j, val in enumerate((ni >> 2, ni & 3, nt >> 2, nt & 3)):
            ids = jnp.where(jnp.logical_and(row == a, lane == j), val, ids)
    common[16:24] = ids.astype(F32)
    shared = jnp.broadcast_to(common[...][None], (LT, 24, TILE))
    rows = jnp.concatenate(
        [text_ref[a] for a in range(PAIRS)] + [cot_ref[a] for a in range(PAIRS)], axis=0
    )
    out_row = iota((TILE, TILE), 0)
    in_row = iota((TILE, TILE), 1)
    perm = one_hot(in_row == (out_row & 7) * LT + (out_row >> 3))
    pieces = mm(perm, rows)
    for c in range(COLS):
        part = pieces[:, c * TILE : (c + 1) * TILE].reshape(LT, 8, TILE)
        out_ref[c * LT : (c + 1) * LT] = jnp.concatenate([shared, part], axis=1).astype(BF)
    for c in range(COLS, DEVS // LT):
        out_ref[c * LT : (c + 1) * LT] = jnp.concatenate(
            [shared, jnp.zeros((LT, 8, TILE), F32)], axis=1
        ).astype(BF)


def pick_kernel(me_ref, got_ref, out_ref, meta_ref, ids_ref, pair_tab):
    rows = DEVS * 8
    got = got_ref[:, 16:32, :].astype(F32)
    ids = got[:, :8].reshape(rows, TILE)
    tab = got[:, 8:].reshape(rows, TILE)
    pair_tab[:, :TILE] = tab.astype(BF)
    pair_tab[:, TILE:] = pltpu.roll(tab, rows - 4, 0).astype(BF)
    owner_col = ids[:, 0:1]
    target_col = ids[:, 2:3] * 8 + ids[:, 3:4]
    eye = one_hot(iota((8, TILE), 0) == iota((8, TILE), 1))
    flat = mm(eye, ids.astype(BF), NT)
    owner_row = flat[0:1]
    local_row = flat[1:2]
    step = 128
    ranks = []
    for b in range(rows // step):
        earlier = iota((step, rows), 1) < iota((step, rows), 0) + b * step
        same = owner_col[b * step : (b + 1) * step] == owner_row
        ranks.append(
            jnp.sum(jnp.where(jnp.logical_and(same, earlier), 1.0, 0.0), axis=1, keepdims=True)
        )
    rank_col = jnp.concatenate(ranks, axis=0)
    lane = iota((rows, TILE), 1)
    with_rank = jnp.where(lane == 4, rank_col, ids).astype(BF)
    ids_ref[...] = with_rank
    flat_rank = mm(one_hot(iota((8, TILE), 1) == 4), with_rank, NT)[0:1]
    key_row = jnp.where(owner_row < 0, -1.0, owner_row * 8 + flat_rank)
    slot_col = (iota((rows, 1), 0)).astype(F32)
    slot_row = (iota((1, rows), 1)).astype(F32)
    step = 256
    for b in range(rows // step):
        block = slice(b * step, (b + 1) * step)
        pushed = mm(one_hot(slot_col[block] == key_row), pair_tab[...])
        pulled = mm(one_hot(target_col[block] == slot_row), pair_tab[:, :TILE])
        out_ref[b * step // 8 : (b + 1) * step // 8] = jnp.concatenate(
            [
                pushed[:, :TILE].reshape(step // 8, 8, TILE),
                pushed[:, TILE:].reshape(step // 8, 8, TILE),
                pulled.reshape(step // 8, 8, TILE),
            ],
            axis=1,
        ).astype(BF)
    mine = (iota((8, rows), 0) + 8 * me_ref[0]).astype(F32) == key_row
    live = jnp.sum(jnp.where(mine, 1.0, 0.0), axis=1, keepdims=True)
    target = jnp.sum(jnp.where(mine, local_row, 0.0), axis=1, keepdims=True)
    meta = jnp.where(live > 0, target, -1.0).astype(jnp.int32)
    meta_ref[...] = jnp.broadcast_to(meta, (8, TILE))


def sum_kernel(ids_ref, got_ref, out_ref):
    rows = DEVS * 8
    ids = ids_ref[...].astype(F32)
    key_col = jnp.where(ids[:, 0:1] < 0, -1.0, ids[:, 0:1] * 8 + ids[:, 4:5])
    eye = one_hot(iota((8, TILE), 0) == iota((8, TILE), 1))
    flat = mm(eye, ids_ref[...], NT)
    target_row = flat[2:3] * 8 + flat[3:4]
    got = got_ref[...].astype(F32)
    push = got[:, :8].reshape(rows, TILE).astype(BF)
    pull = got[:, 8:].reshape(rows, TILE).astype(BF)
    slot_col = (iota((rows, 1), 0)).astype(F32)
    slot_row = (iota((1, rows), 1)).astype(F32)
    step = 256
    for b in range(rows // step):
        block = slice(b * step, (b + 1) * step)
        total = mm(one_hot(key_col[block] == slot_row), push)
        total += mm(one_hot(slot_col[block] == target_row), pull)
        out_ref[b * step // 8 : (b + 1) * step // 8] = total.reshape(step // 8, 8, TILE).astype(BF)


def join_kernel(own_ref, got_ref, out_ref):
    parts = []
    for c in range(COLS):
        got = got_ref[c * LT : (c + 1) * LT].astype(F32)
        parts.append(got.reshape(TILE, TILE).astype(BF))
    pieces = jnp.concatenate(parts, axis=1)
    out_row = iota((PAIRS * LT, TILE), 0)
    in_row = iota((PAIRS * LT, TILE), 1)
    perm = one_hot(in_row == (out_row & 15) * 8 + (out_row >> 4))
    total = own_ref[...] + mm(perm, pieces)
    out_ref[...] = total.astype(BF).reshape(PAIRS, LT, D)


def head_mask():
    return one_hot((iota((GR, GW), 0) >> 4) == (iota((GR, GW), 1) >> 6))


def spread(rows, mask):
    return jnp.concatenate([rows] * GROUP, axis=0) * mask


def fold(full):
    head = iota((LT, GW), 1) >> 6
    out = full[0:LT]
    for h in range(1, GROUP):
        out = jnp.where(head == h, full[h * LT : (h + 1) * LT], out)
    return out


def attend(i, target, keys, values, query, weights, probs, context):
    mask = head_mask()
    at = pl.ds(pl.multiple_of(i * LT, LT), LT)
    lane = iota((GR, LIP), 1)
    for g in range(GROUPS):
        cols = slice(g * GW, (g + 1) * GW)
        scores = mm(spread(query[at, cols], mask), keys[target, :, cols], NT) * INV_ROOT
        scores = jnp.where(lane < LI, scores, -1e30)
        w = jnp.exp(scores - jnp.max(scores, axis=1, keepdims=True))
        w = w / jnp.sum(w, axis=1, keepdims=True)
        half = w.astype(BF)
        rows = slice(g * GR, (g + 1) * GR)
        weights[i, rows, :] = w
        probs[i, rows, :] = half
        context[at, cols] = fold(mm(half, values[target, :, cols])).astype(BF)


def attend_back(i, target, keys, values, d_context, weights, d_scores, d_query):
    mask = head_mask()
    at = pl.ds(pl.multiple_of(i * LT, LT), LT)
    for g in range(GROUPS):
        cols = slice(g * GW, (g + 1) * GW)
        rows = slice(g * GR, (g + 1) * GR)
        d_probs = mm(spread(d_context[at, cols], mask), values[target, :, cols], NT)
        w = weights[i, rows, :]
        ds = w * (d_probs - jnp.sum(w * d_probs, axis=1, keepdims=True)) * INV_ROOT
        ds = ds.astype(BF)
        d_scores[i, rows, :] = ds
        d_query[at, cols] = fold(mm(ds, keys[target, :, cols])).astype(BF)


def norm_back(summed, cot, gain):
    centred = summed - jnp.mean(summed, axis=1, keepdims=True)
    inv_sigma = lax.rsqrt(jnp.mean(centred * centred, axis=1, keepdims=True) + NORM_EPS)
    normed = centred * inv_sigma
    gz = cot * gain
    return inv_sigma * (
        gz
        - jnp.mean(gz, axis=1, keepdims=True)
        - normed * jnp.mean(gz * normed, axis=1, keepdims=True)
    )


def own_kernel(
    text_ref, cot_ref, keys, values, wq_ref, wo_ref, gain_ref,
    grad_ref, d_scores, probs, query, d_context,
    weights, context, d_query,
):
    texts = text_ref[...].reshape(PAIRS * LT, D)
    query[...] = mm(texts, wq_ref[...]).astype(BF)
    for i in range(PAIRS):
        attend(i, i, keys, values, query, weights, probs, context)
    summed = mm(context[...], wo_ref[...]) + texts.astype(F32)
    cots = cot_ref[...].reshape(PAIRS * LT, D).astype(F32)
    d_summed = norm_back(summed, cots, gain_ref[...])
    d_context[...] = mm(d_summed.astype(BF), wo_ref[...], NT).astype(BF)
    for i in range(PAIRS):
        attend_back(i, i, keys, values, d_context, weights, d_scores, d_query)
    grad_ref[...] = d_summed + mm(d_query[...], wq_ref[...], NT)


def guest_kernel(
    meta, got_ref, cot_ref, keys, values, wq_ref, wo_ref, gain_ref,
    out_ref, d_scores, probs, query, d_context,
    weights, context, d_query, texts, cots, d_summed_ref,
):
    count = PUSH + PAIRS
    parts = []
    for c in range(COLS):
        got = got_ref[c * LT : (c + 1) * LT].astype(F32)
        parts.append(got.reshape(LT * 24, TILE).astype(BF))
    pieces = jnp.concatenate(parts, axis=1)
    out_row = iota((20 * LT, 24 * LT), 0)
    in_row = iota((20 * LT, 24 * LT), 1)
    perm = one_hot(in_row == (out_row & 15) * 24 + (out_row >> 4))
    rows = mm(perm, pieces)
    push_rows = PUSH * LT
    texts[:push_rows] = rows[:push_rows].astype(BF)
    texts[push_rows:] = rows[2 * push_rows :].astype(BF)
    cots[:push_rows] = rows[push_rows : 2 * push_rows].astype(BF)
    cots[push_rows:] = cot_ref[...].reshape(PAIRS * LT, D)
    query[...] = mm(texts[...], wq_ref[...]).astype(BF)

    def targets(i):
        return jnp.maximum(meta[i, 0], 0)

    def forward(s, carry):
        for u in range(2):
            i = s * 2 + u
            attend(i, targets(i), keys, values, query, weights, probs, context)
        return carry

    def backward(s, carry):
        for u in range(2):
            i = s * 2 + u
            attend_back(i, targets(i), keys, values, d_context, weights, d_scores, d_query)
        return carry

    lax.fori_loop(0, PUSH // 2, forward, 0)
    for j in range(PAIRS):
        attend(PUSH + j, j, keys, values, query, weights, probs, context)
    summed = mm(context[...], wo_ref[...]) + texts[...].astype(F32)
    d_summed = norm_back(summed, cots[...].astype(F32), gain_ref[...])
    d_summed_ref[...] = d_summed
    d_context[...] = mm(d_summed.astype(BF), wo_ref[...], NT).astype(BF)
    lax.fori_loop(0, PUSH // 2, backward, 0)
    for j in range(PAIRS):
        attend_back(PUSH + j, j, keys, values, d_context, weights, d_scores, d_query)
    grads = (d_summed_ref[...] + mm(d_query[...], wq_ref[...], NT)).astype(BF)
    out_row = iota((LT * 16, count * LT), 0)
    in_row = iota((LT * 16, count * LT), 1)
    perm = one_hot(in_row == (out_row & 15) * LT + (out_row >> 4))
    back = mm(perm, grads).astype(BF)
    for c in range(COLS):
        out_ref[c * LT : (c + 1) * LT] = back[:, c * TILE : (c + 1) * TILE].reshape(LT, 16, TILE)
    out_ref[PIECES:] = jnp.zeros((DEVS - PIECES, 16, TILE), BF)


def project_kernel(image_ref, wk_ref, wv_ref, keys, values, padded):
    padded[...] = jnp.zeros_like(padded)
    zero = jnp.zeros((LIP - LIR, D), BF)
    for t in range(PAIRS):
        padded[0:LI] = image_ref[t]
        rows = padded[...]
        keys[t, 0:LIR] = mm(rows, wk_ref[...]).astype(BF)
        values[t, 0:LIR] = mm(rows, wv_ref[...]).astype(BF)
        keys[t, LIR:] = zero
        values[t, LIR:] = zero


def image_kernel(
    meta, own_ds, own_p, own_q, own_dc, ds, p, q, dc, wk_ref, wv_ref, out_ref, d_keys, d_values
):
    mask = head_mask()

    def term(scores, rows):
        return mm(scores[:, :LIR], rows, TN)

    for t in range(PAIRS):
        at = slice(t * LT, (t + 1) * LT)
        pat = slice((PUSH + t) * LT, (PUSH + t + 1) * LT)
        for g in range(GROUPS):
            cols = slice(g * GW, (g + 1) * GW)
            rows = slice(g * GR, (g + 1) * GR)
            d_keys[t, :, cols] = term(
                jnp.concatenate([own_ds[t, rows, :], ds[PUSH + t, rows, :]], axis=0),
                jnp.concatenate(
                    [spread(own_q[at, cols], mask), spread(q[pat, cols], mask)], axis=0
                ),
            )
            d_values[t, :, cols] = term(
                jnp.concatenate([own_p[t, rows, :], p[PUSH + t, rows, :]], axis=0),
                jnp.concatenate(
                    [spread(own_dc[at, cols], mask), spread(dc[pat, cols], mask)], axis=0
                ),
            )

    def visit(i, carry):
        target = meta[i, 0]

        @pl.when(target >= 0)
        def _():
            at = pl.ds(pl.multiple_of(i * LT, LT), LT)
            for g in range(GROUPS):
                cols = slice(g * GW, (g + 1) * GW)
                rows = slice(g * GR, (g + 1) * GR)
                d_keys[target, :, cols] += term(ds[i, rows, :], spread(q[at, cols], mask))
                d_values[target, :, cols] += term(p[i, rows, :], spread(dc[at, cols], mask))

        return carry

    lax.fori_loop(0, PUSH, visit, 0)
    for t in range(PAIRS):
        total = mm(d_keys[t].astype(BF), wk_ref[...], NT)
        total += mm(d_values[t].astype(BF), wv_ref[...], NT)
        out_ref[t] = total.astype(BF)[:LI]


def contrast_kernel(got_ref, tf_ref, if_ref, dt_ref, di_ref, *, me_ref):
    rows = DEVS * 8
    got = got_ref[:, 0:16, :].astype(F32)
    feats = jnp.concatenate(
        [got[:, :8].reshape(rows, TILE), got[:, 8:].reshape(rows, TILE)], axis=1
    ).astype(BF)
    total = DEVS * PAIRS
    out_row = iota((total, rows), 0)
    in_row = iota((total, rows), 1)
    place = (out_row >> 2) * 8 + (out_row & 3)
    texts = mm(one_hot(in_row == place), feats).astype(BF)
    images = mm(one_hot(in_row == place + 4), feats).astype(BF)
    similar = mm(texts, images, NT) * SIM_SCALE
    row_peak = jnp.max(similar, axis=1, keepdims=True)
    col_peak = jnp.max(similar, axis=0, keepdims=True)
    row_lse = row_peak + jnp.log(jnp.sum(jnp.exp(similar - row_peak), axis=1, keepdims=True))
    col_lse = col_peak + jnp.log(jnp.sum(jnp.exp(similar - col_peak), axis=0, keepdims=True))
    d_similar = 0.5 * jnp.exp(similar - row_lse) + 0.5 * jnp.exp(similar - col_lse)
    diagonal = iota((total, total), 0) == iota((total, total), 1)
    d_similar = d_similar - jnp.where(diagonal, 1.0, 0.0)
    base = me_ref[0] * PAIRS
    mine = iota((8, total), 1) == iota((8, total), 0) + base
    pick = jnp.where(jnp.logical_and(mine, iota((8, total), 0) < PAIRS), 1.0, 0.0)
    high = lax.Precision.HIGHEST
    d_rows = lax.dot_general(pick, d_similar, NN, precision=high, preferred_element_type=F32)
    d_cols = lax.dot_general(pick, d_similar, NT, precision=high, preferred_element_type=F32)
    d_text = lax.dot_general(
        d_rows, images.astype(F32), NN, precision=high, preferred_element_type=F32
    )
    d_image = lax.dot_general(
        d_cols, texts.astype(F32), NN, precision=high, preferred_element_type=F32
    )
    dt_ref[...] = SIM_SCALE * d_text[:PAIRS]
    di_ref[...] = SIM_SCALE * d_image[:PAIRS]


def contrast_entry(me_ref, got_ref, dt_ref, di_ref):
    contrast_kernel(got_ref, None, None, dt_ref, di_ref, me_ref=me_ref)


def call(kernel, outs, smem, args, scratch=(), flops=0, name=None):
    vmem = pl.BlockSpec(memory_space=pltpu.VMEM)
    scalar = pl.BlockSpec(memory_space=pltpu.SMEM)
    shapes = [jax.ShapeDtypeStruct(s, d) for s, d in outs]
    size = sum(a.size * a.dtype.itemsize for a in args)
    size += sum(math.prod(s.shape) * s.dtype.itemsize for s in shapes)
    return pl.pallas_call(
        kernel,
        out_shape=shapes,
        in_specs=[scalar] * smem + [vmem] * (len(args) - smem),
        out_specs=[vmem] * len(shapes),
        scratch_shapes=list(scratch),
        compiler_params=pltpu.CompilerParams(vmem_limit_bytes=VMEM_LIMIT),
        cost_estimate=pl.CostEstimate(flops=flops, bytes_accessed=size, transcendentals=0),
        name=name,
    )(*args)


def exchange(x):
    return lax.all_to_all(x, "dp", split_axis=0, concat_axis=0, tiled=True)


def on_device(
    text_states, image_states, cot_positive, cot_neg_image, cot_neg_text,
    w_query, w_key, w_value, w_out, ln_gain, neg_image, neg_text, text_feat, image_feat,
):
    me = lax.axis_index("dp").astype(jnp.int32).reshape(1)
    gain = ln_gain.reshape(1, D)
    count = PUSH + PAIRS
    (send,) = call(
        pack_kernel,
        [((DEVS, 32, TILE), BF)],
        2,
        (neg_image, neg_text, text_states, cot_neg_image, text_feat, image_feat),
        [pltpu.VMEM((24, TILE), F32)],
        name="pack",
    )
    got = exchange(send)
    keys, values = call(
        project_kernel,
        [((PAIRS, LIP, D), BF)] * 2,
        0,
        (image_states, w_key, w_value),
        [pltpu.VMEM((LIR, D), BF)],
        flops=4 * PAIRS * LIR * D * D,
        name="project",
    )
    own_grad, own_ds, own_p, own_q, own_dc = call(
        own_kernel,
        [
            ((PAIRS * LT, D), F32),
            ((PAIRS, H * LT, LIP), BF),
            ((PAIRS, H * LT, LIP), BF),
            ((PAIRS * LT, D), BF),
            ((PAIRS * LT, D), BF),
        ],
        0,
        (text_states, cot_positive, keys, values, w_query, w_out, gain),
        [
            pltpu.VMEM((PAIRS, H * LT, LIP), F32),
            pltpu.VMEM((PAIRS * LT, D), BF),
            pltpu.VMEM((PAIRS * LT, D), BF),
        ],
        flops=8 * PAIRS * LT * D * D * 4,
        name="own",
    )
    send, meta, ids = call(
        pick_kernel,
        [((DEVS, 24, TILE), BF), ((8, TILE), jnp.int32), ((DEVS * 8, TILE), BF)],
        1,
        (me, got),
        [pltpu.VMEM((DEVS * 8, 2 * TILE), BF)],
        name="pick",
    )
    got_rows = exchange(send)
    d_text_feat, d_image_feat = call(
        contrast_entry,
        [((PAIRS, E), F32), ((PAIRS, E), F32)],
        1,
        (me, got),
        flops=8 * 512 * 512 * 256,
        name="contrast",
    )
    send, ds, p, q, dc = call(
        guest_kernel,
        [
            ((DEVS, 16, TILE), BF),
            ((count, H * LT, LIP), BF),
            ((count, H * LT, LIP), BF),
            ((count * LT, D), BF),
            ((count * LT, D), BF),
        ],
        1,
        (meta, got_rows, cot_neg_text, keys, values, w_query, w_out, gain),
        [
            pltpu.VMEM((count, H * LT, LIP), F32),
            pltpu.VMEM((count * LT, D), BF),
            pltpu.VMEM((count * LT, D), BF),
            pltpu.VMEM((count * LT, D), BF),
            pltpu.VMEM((count * LT, D), BF),
            pltpu.VMEM((count * LT, D), F32),
        ],
        flops=8 * count * LT * D * D * 4,
        name="guest",
    )
    got_back = exchange(send)
    (d_image,) = call(
        image_kernel,
        [((PAIRS, LI, D), BF)],
        1,
        (meta, own_ds, own_p, own_q, own_dc, ds, p, q, dc, w_key, w_value),
        [pltpu.VMEM((PAIRS, LIR, D), F32), pltpu.VMEM((PAIRS, LIR, D), F32)],
        flops=8 * PAIRS * LIR * D * D,
        name="image",
    )
    (send,) = call(sum_kernel, [((DEVS, 8, TILE), BF)], 0, (ids, got_back), name="sum")
    got_sum = exchange(send)
    (d_text,) = call(join_kernel, [((PAIRS, LT, D), BF)], 0, (own_grad, got_sum), name="join")
    return (d_text, d_image, d_text_feat, d_image_feat)


def solution(mesh):
    return jax.shard_map(
        on_device,
        mesh=mesh,
        in_specs=(
            P("dp", None, None),
            P("dp", None, None),
            P("dp", None, None),
            P("dp", None, None),
            P("dp", None, None),
            P(),
            P(),
            P(),
            P(),
            P(),
            P("dp"),
            P("dp"),
            P("dp", None),
            P("dp", None),
        ),
        out_specs=(P("dp", None, None), P("dp", None, None), P("dp", None), P("dp", None)),
        check_vma=False,
    )
```

```python
import math

import jax
import jax.numpy as jnp
from jax import lax
from jax.experimental import pallas as pl
from jax.experimental.pallas import tpu as pltpu
from jax.sharding import PartitionSpec as P

D = 768
H = 12
E = 256
LT = 16
LI = 197
PAIRS = 4
DEVS = 128
TILE = 128
COLS = D // TILE
PIECES = COLS * LT
LIR = 208
GROUP = 4
GROUPS = H // GROUP
GW = D // GROUPS
GR = GROUP * LT
INV_ROOT = 1.0 / math.sqrt(D // H)
NORM_EPS = 1e-06
SIM_SCALE = 3.0 / math.sqrt(E)
PUSH = 2 * PAIRS
BF = jnp.bfloat16
F32 = jnp.float32
VMEM_LIMIT = 56 * 1024 * 1024

NN = (((1,), (0,)), ((), ()))
NT = (((1,), (1,)), ((), ()))
TN = (((0,), (0,)), ((), ()))


def mm(a, b, dims=NN):
    return lax.dot_general(a, b, dims, preferred_element_type=F32)


def iota(shape, dim):
    return lax.broadcasted_iota(jnp.int32, shape, dim)


def one_hot(mask):
    return jnp.where(mask, 1.0, 0.0).astype(BF)


def pack_kernel(ni_in, nt_in, tf_in, if_in, text_in, cot_in, out, feat, feats):
    out_row = iota((TILE, TILE), 0)
    in_row = iota((TILE, TILE), 1)
    perm = one_hot(in_row == (out_row & 7) * LT + (out_row >> 3))
    row = iota((8, TILE), 0)
    lane = iota((8, TILE), 1)
    ni_ref, nt_ref = ni_in(), nt_in()
    ids = jnp.full((8, TILE), -1, jnp.int32)
    for a in range(PAIRS):
        ni = ni_ref[a]
        nt = nt_ref[a]
        for j, val in enumerate((ni >> 2, ni & 3, nt >> 2, nt & 3)):
            ids = jnp.where(jnp.logical_and(row == a, lane == j), val, ids)
    shared = jnp.broadcast_to(ids.astype(F32)[None], (LT, 8, TILE))
    tf = tf_in()[...].astype(F32)
    im = if_in()[...].astype(F32)
    feats[0:4] = tf[:, :TILE]
    feats[4:8] = im[:, :TILE]
    feats[8:12] = tf[:, TILE:]
    feats[12:16] = im[:, TILE:]
    feat.ref[0:16] = feats[...].astype(BF)
    feat.ref[16:32] = jnp.zeros((16, TILE), BF)
    feat.send()
    rows = jnp.concatenate([text_in()[...], cot_in()[...]], axis=0).reshape(TILE, D)
    pieces = mm(perm, rows)
    for c in range(COLS):
        part = pieces[:, c * TILE : (c + 1) * TILE].reshape(LT, 8, TILE)
        out.ref[c * LT : (c + 1) * LT] = jnp.concatenate([shared, part], axis=1).astype(BF)
    for c in range(COLS, DEVS // LT):
        out.ref[c * LT : (c + 1) * LT] = jnp.concatenate(
            [shared, jnp.zeros((LT, 8, TILE), F32)], axis=1
        ).astype(BF)
    out.send()


def pick_kernel(me_in, got_in, out, meta_out, ids_out, pair_tab):
    rows = DEVS * 8
    got = got_in()[...].astype(F32)
    ids = got[:, :8].reshape(rows, TILE)
    tab = got[:, 8:].reshape(rows, TILE)
    pair_tab[:, :TILE] = tab.astype(BF)
    pair_tab[:, TILE:] = pltpu.roll(tab, rows - 4, 0).astype(BF)
    owner_col = ids[:, 0:1]
    target_col = ids[:, 2:3] * 8 + ids[:, 3:4]
    eye = one_hot(iota((8, TILE), 0) == iota((8, TILE), 1))
    flat = mm(eye, ids.astype(BF), NT)
    owner_row = flat[0:1]
    local_row = flat[1:2]
    step = 128
    ranks = []
    for b in range(rows // step):
        earlier = iota((step, rows), 1) < iota((step, rows), 0) + b * step
        same = owner_col[b * step : (b + 1) * step] == owner_row
        ranks.append(
            jnp.sum(jnp.where(jnp.logical_and(same, earlier), 1.0, 0.0), axis=1, keepdims=True)
        )
    rank_col = jnp.concatenate(ranks, axis=0)
    lane = iota((rows, TILE), 1)
    with_rank = jnp.where(lane == 4, rank_col, ids).astype(BF)
    ids_out.ref[...] = with_rank
    ids_out.send()
    flat_rank = mm(one_hot(iota((8, TILE), 1) == 4), with_rank, NT)[0:1]
    key_row = jnp.where(owner_row < 0, -1.0, owner_row * 8 + flat_rank)
    slot_col = (iota((rows, 1), 0)).astype(F32)
    slot_row = (iota((1, rows), 1)).astype(F32)
    step = 256
    for b in range(rows // step):
        block = slice(b * step, (b + 1) * step)
        pushed = mm(one_hot(slot_col[block] == key_row), pair_tab[...])
        pulled = mm(one_hot(target_col[block] == slot_row), pair_tab[:, :TILE])
        out.ref[b * step // 8 : (b + 1) * step // 8] = jnp.concatenate(
            [
                pushed[:, :TILE].reshape(step // 8, 8, TILE),
                pushed[:, TILE:].reshape(step // 8, 8, TILE),
                pulled.reshape(step // 8, 8, TILE),
            ],
            axis=1,
        ).astype(BF)
    out.send()
    mine = (iota((8, rows), 0) + 8 * me_in()[0]).astype(F32) == key_row
    live = jnp.sum(jnp.where(mine, 1.0, 0.0), axis=1, keepdims=True)
    target = jnp.sum(jnp.where(mine, local_row, 0.0), axis=1, keepdims=True)
    meta = jnp.where(live > 0, target, -1.0).astype(jnp.int32)
    meta_out.ref[...] = jnp.broadcast_to(meta, (8, TILE))
    meta_out.send()


def sum_kernel(ids_in, got_in, out):
    rows = DEVS * 8
    ids_ref = ids_in()
    ids = ids_ref[...].astype(F32)
    key_col = jnp.where(ids[:, 0:1] < 0, -1.0, ids[:, 0:1] * 8 + ids[:, 4:5])
    eye = one_hot(iota((8, TILE), 0) == iota((8, TILE), 1))
    flat = mm(eye, ids_ref[...], NT)
    target_row = flat[2:3] * 8 + flat[3:4]
    got = got_in()[...].astype(F32)
    push = got[:, :8].reshape(rows, TILE).astype(BF)
    pull = got[:, 8:].reshape(rows, TILE).astype(BF)
    slot_col = (iota((rows, 1), 0)).astype(F32)
    slot_row = (iota((1, rows), 1)).astype(F32)
    step = 256
    for b in range(rows // step):
        block = slice(b * step, (b + 1) * step)
        total = mm(one_hot(key_col[block] == slot_row), push)
        total += mm(one_hot(slot_col[block] == target_row), pull)
        out.ref[b * step // 8 : (b + 1) * step // 8] = total.reshape(step // 8, 8, TILE).astype(BF)
    out.send()


def join_kernel(own_in, got_in, out):
    parts = []
    got_ref = got_in()
    for c in range(COLS):
        got = got_ref[c * LT : (c + 1) * LT].astype(F32)
        parts.append(got.reshape(TILE, TILE).astype(BF))
    pieces = jnp.concatenate(parts, axis=1)
    out_row = iota((PAIRS * LT, TILE), 0)
    in_row = iota((PAIRS * LT, TILE), 1)
    perm = one_hot(in_row == (out_row & 15) * 8 + (out_row >> 4))
    total = own_in()[...] + mm(perm, pieces)
    out.ref[...] = total.astype(BF).reshape(PAIRS, LT, D)
    out.send()


def head_mask():
    return one_hot((iota((GR, GW), 0) >> 4) == (iota((GR, GW), 1) >> 6))


def spread(rows, mask):
    return jnp.concatenate([rows] * GROUP, axis=0) * mask


def fold(full):
    head = iota((LT, GW), 1) >> 6
    out = full[0:LT]
    for h in range(1, GROUP):
        out = jnp.where(head == h, full[h * LT : (h + 1) * LT], out)
    return out


def parts_of(items, targets):
    for i, target in zip(items, targets):
        at = pl.ds(pl.multiple_of(i * LT, LT), LT)
        for g in range(GROUPS):
            yield i, target, at, slice(g * GW, (g + 1) * GW), slice(g * GR, (g + 1) * GR)


def attend(items, targets, keys_t, values, query, weights, probs, context):
    mask = head_mask()
    lane = iota((GR, LIR), 1)
    work = list(parts_of(items, targets))
    scores = []
    for i, target, at, cols, rows in work:
        s = mm(spread(query[at, cols], mask), keys_t[target, cols, :]) * INV_ROOT
        scores.append(jnp.where(lane < LI, s, -1e30))
    halves = []
    for (i, target, at, cols, rows), s in zip(work, scores):
        w = jnp.exp(s - jnp.max(s, axis=1, keepdims=True))
        w = w / jnp.sum(w, axis=1, keepdims=True)
        half = w.astype(BF)
        weights[i, rows, :] = w
        probs[i, rows, :] = half
        halves.append(half)
    for (i, target, at, cols, rows), half in zip(work, halves):
        context[at, cols] = fold(mm(half, values[target, :, cols])).astype(BF)


def attend_back(items, targets, keys, values_t, d_context, weights, d_scores, d_query):
    mask = head_mask()
    work = list(parts_of(items, targets))
    d_probs = []
    for i, target, at, cols, rows in work:
        d_probs.append(mm(spread(d_context[at, cols], mask), values_t[target, cols, :]))
    halves = []
    for (i, target, at, cols, rows), dp in zip(work, d_probs):
        w = weights[i, rows, :]
        ds = w * (dp - jnp.sum(w * dp, axis=1, keepdims=True)) * INV_ROOT
        ds = ds.astype(BF)
        d_scores[i, rows, :] = ds
        halves.append(ds)
    for (i, target, at, cols, rows), ds in zip(work, halves):
        d_query[at, cols] = fold(mm(ds, keys[target, :, cols])).astype(BF)


def norm_back(summed, cot, gain):
    centred = summed - jnp.mean(summed, axis=1, keepdims=True)
    inv_sigma = lax.rsqrt(jnp.mean(centred * centred, axis=1, keepdims=True) + NORM_EPS)
    normed = centred * inv_sigma
    gz = cot * gain
    return inv_sigma * (
        gz
        - jnp.mean(gz, axis=1, keepdims=True)
        - normed * jnp.mean(gz * normed, axis=1, keepdims=True)
    )


def front_kernel(
    image_in, wk_in, wv_in, text_in, wq_in, wo_in, gain_in, cot_in,
    keys_o, values_o, keys_t_o, values_t_o, wo_t_o, wq_t_o,
    grad_o, d_scores, probs, query, d_context,
    weights, context, d_query, padded,
):
    keys, values, keys_t, values_t = (o.ref for o in (keys_o, values_o, keys_t_o, values_t_o))
    image = image_in()
    padded[...] = jnp.zeros_like(padded)
    for t in range(PAIRS):
        padded[0:LI] = image[t]
        rows = padded[...]
        for w_in, plain, turned in ((wk_in, keys, keys_t), (wv_in, values, values_t)):
            made = mm(rows, w_in()[...]).astype(BF)
            plain[t] = made
            turned[t] = made.T
    for o in (keys_o, values_o, keys_t_o, values_t_o):
        o.send()
    texts = text_in()[...].reshape(PAIRS * LT, D)
    wq, wo = wq_in(), wo_in()
    wo_t_o.ref[...] = wo[...].T
    wo_t_o.send()
    wq_t_o.ref[...] = wq[...].T
    wq_t_o.send()
    query.ref[...] = mm(texts, wq[...]).astype(BF)
    query.send()
    every = list(range(PAIRS))
    attend(every, every, keys_t, values, query.ref, weights, probs.ref, context)
    probs.send()
    summed = mm(context[...], wo[...]) + texts.astype(F32)
    cots = cot_in()[...].reshape(PAIRS * LT, D).astype(F32)
    d_summed = norm_back(summed, cots, gain_in()[...])
    d_context.ref[...] = mm(d_summed.astype(BF), wo_t_o.ref[...]).astype(BF)
    d_context.send()
    attend_back(every, every, keys, values_t, d_context.ref, weights, d_scores.ref, d_query)
    d_scores.send()
    grad_o.ref[...] = d_summed + mm(d_query[...], wq_t_o.ref[...])
    grad_o.send()


def guest_kernel(
    got_in, meta_in, cot_in, wq_in, keys_t_in, values_in, wo_in, gain_in,
    wo_t_in, values_t_in, keys_in, wq_t_in,
    out, query, probs, d_context, d_scores,
    weights, context, d_query, texts, cots, d_summed_ref,
):
    count = PUSH + PAIRS
    out_row = iota((20 * LT, 24 * LT), 0)
    in_row = iota((20 * LT, 24 * LT), 1)
    perm = one_hot(in_row == (out_row & 15) * 24 + (out_row >> 4))
    got_ref = got_in()
    parts = []
    for c in range(COLS):
        got = got_ref[c * LT : (c + 1) * LT].astype(F32)
        parts.append(got.reshape(LT * 24, TILE).astype(BF))
    pieces = jnp.concatenate(parts, axis=1)
    rows = mm(perm, pieces)
    push_rows = PUSH * LT
    texts[:push_rows] = rows[:push_rows].astype(BF)
    texts[push_rows:] = rows[2 * push_rows :].astype(BF)
    cots[:push_rows] = rows[push_rows : 2 * push_rows].astype(BF)
    cots[push_rows:] = cot_in()[...].reshape(PAIRS * LT, D)
    query.ref[...] = mm(texts[...], wq_in()[...]).astype(BF)
    query.send()
    meta = meta_in()
    own = list(range(PAIRS))
    pulled = [PUSH + j for j in own]
    keys_t, values = keys_t_in(), values_in()

    def batch(s):
        items = [s * PAIRS + u for u in range(PAIRS)]
        return items, [jnp.maximum(meta[i, 0], 0) for i in items]

    def forward(s, carry):
        attend(*batch(s), keys_t, values, query.ref, weights, probs.ref, context)
        return carry

    lax.fori_loop(0, PUSH // PAIRS, forward, 0)
    attend(pulled, own, keys_t, values, query.ref, weights, probs.ref, context)
    probs.send()
    summed = mm(context[...], wo_in()[...]) + texts[...].astype(F32)
    d_summed = norm_back(summed, cots[...].astype(F32), gain_in()[...])
    d_summed_ref[...] = d_summed
    d_context.ref[...] = mm(d_summed.astype(BF), wo_t_in()[...]).astype(BF)
    d_context.send()
    keys, values_t = keys_in(), values_t_in()

    def backward(s, carry):
        attend_back(*batch(s), keys, values_t, d_context.ref, weights, d_scores.ref, d_query)
        return carry

    lax.fori_loop(0, PUSH // PAIRS, backward, 0)
    attend_back(pulled, own, keys, values_t, d_context.ref, weights, d_scores.ref, d_query)
    d_scores.send()
    grads = (d_summed_ref[...] + mm(d_query[...], wq_t_in()[...])).astype(BF)
    out_row = iota((LT * 16, count * LT), 0)
    in_row = iota((LT * 16, count * LT), 1)
    perm = one_hot(in_row == (out_row & 15) * LT + (out_row >> 4))
    back = mm(perm, grads).astype(BF)
    for c in range(COLS):
        out.ref[c * LT : (c + 1) * LT] = back[:, c * TILE : (c + 1) * TILE].reshape(LT, 16, TILE)
    out.ref[PIECES:] = jnp.zeros((DEVS - PIECES, 16, TILE), BF)
    out.send()


def image_kernel(
    own_ds_in, own_q_in, ds_in, q_in, own_p_in, own_dc_in, p_in, dc_in, meta_in, wk_in, wv_in,
    out, d_keys, d_values,
):
    mask = head_mask()

    def term(scores, rows):
        return mm(scores, rows, TN)

    sides = (
        (d_keys, own_ds_in(), own_q_in(), ds_in(), q_in()),
        (d_values, own_p_in(), own_dc_in(), p_in(), dc_in()),
    )
    for t in range(PAIRS):
        at = slice(t * LT, (t + 1) * LT)
        pat = slice((PUSH + t) * LT, (PUSH + t + 1) * LT)
        for g in range(GROUPS):
            cols = slice(g * GW, (g + 1) * GW)
            rows = slice(g * GR, (g + 1) * GR)
            for total, own_left, own_right, left, right in sides:
                total[t, :, cols] = term(
                    jnp.concatenate([own_left[t, rows, :], left[PUSH + t, rows, :]], axis=0),
                    jnp.concatenate(
                        [spread(own_right[at, cols], mask), spread(right[pat, cols], mask)], axis=0
                    ),
                )
    meta = meta_in()

    def visit(i, carry):
        target = meta[i, 0]

        @pl.when(target >= 0)
        def _():
            at = pl.ds(pl.multiple_of(i * LT, LT), LT)
            for g in range(GROUPS):
                cols = slice(g * GW, (g + 1) * GW)
                rows = slice(g * GR, (g + 1) * GR)
                for total, _, _, left, right in sides:
                    total[target, :, cols] += term(left[i, rows, :], spread(right[at, cols], mask))

        return carry

    lax.fori_loop(0, PUSH, visit, 0)
    wk, wv = wk_in()[...].T, wv_in()[...].T
    for t in range(PAIRS):
        total = mm(d_keys[t].astype(BF), wk) + mm(d_values[t].astype(BF), wv)
        out.ref[t] = total.astype(BF)[:LI]
    out.send()


def contrast_kernel(me_in, got_in, d_text_o, d_image_o):
    rows = DEVS * 8
    got = got_in()[...].reshape(DEVS, 32, TILE)[:, :16].astype(F32)
    feats = jnp.concatenate(
        [got[:, :8].reshape(rows, TILE), got[:, 8:].reshape(rows, TILE)], axis=1
    ).astype(BF)
    total = DEVS * PAIRS
    out_row = iota((total, rows), 0)
    in_row = iota((total, rows), 1)
    place = (out_row >> 2) * 8 + (out_row & 3)
    texts = mm(one_hot(in_row == place), feats).astype(BF)
    images = mm(one_hot(in_row == place + 4), feats).astype(BF)
    similar = mm(texts, images, NT) * SIM_SCALE
    row_peak = jnp.max(similar, axis=1, keepdims=True)
    col_peak = jnp.max(similar, axis=0, keepdims=True)
    row_lse = row_peak + jnp.log(jnp.sum(jnp.exp(similar - row_peak), axis=1, keepdims=True))
    col_lse = col_peak + jnp.log(jnp.sum(jnp.exp(similar - col_peak), axis=0, keepdims=True))
    d_similar = 0.5 * jnp.exp(similar - row_lse) + 0.5 * jnp.exp(similar - col_lse)
    diagonal = iota((total, total), 0) == iota((total, total), 1)
    d_similar = d_similar - jnp.where(diagonal, 1.0, 0.0)
    base = me_in()[0] * PAIRS
    mine = iota((8, total), 1) == iota((8, total), 0) + base
    pick = jnp.where(jnp.logical_and(mine, iota((8, total), 0) < PAIRS), 1.0, 0.0)
    high = lax.Precision.HIGHEST
    d_rows = lax.dot_general(pick, d_similar, NN, precision=high, preferred_element_type=F32)
    d_cols = lax.dot_general(pick, d_similar, NT, precision=high, preferred_element_type=F32)
    d_text = lax.dot_general(
        d_rows, images.astype(F32), NN, precision=high, preferred_element_type=F32
    )
    d_image = lax.dot_general(
        d_cols, texts.astype(F32), NN, precision=high, preferred_element_type=F32
    )
    d_text_o.ref[...] = SIM_SCALE * d_text[:PAIRS]
    d_text_o.send()
    d_image_o.ref[...] = SIM_SCALE * d_image[:PAIRS]
    d_image_o.send()


class Loaded:
    def __init__(self, src, dst, sem):
        self.copy = pltpu.make_async_copy(src, dst, sem)
        self.copy.start()
        self.buffer = dst
        self.waited = False

    def __call__(self):
        if not self.waited:
            self.copy.wait()
            self.waited = True
        return self.buffer


class Stored:
    def __init__(self, ref, dst, sem):
        self.ref = ref
        self.copy = pltpu.make_async_copy(ref, dst, sem)

    def send(self):
        self.copy.start()


def call(kernel, outs, args, scratch=(), flops=0, name=None, scalars=()):
    shapes = [jax.ShapeDtypeStruct(s, d) for s, d in outs]
    n, m = len(args), len(outs)
    size = sum(a.size * a.dtype.itemsize for a in args)
    size += sum(math.prod(s.shape) * s.dtype.itemsize for s in shapes)

    def body(*refs):
        arrays, buffers = refs[: n + m], refs[n + m : 2 * (n + m)]
        sems, rest = refs[2 * (n + m)], refs[2 * (n + m) + 1 :]
        loads = [Loaded(arrays[k], buffers[k], sems.at[k]) for k in range(n)]
        stores = [Stored(buffers[k], arrays[k], sems.at[k]) for k in range(n, n + m)]
        kernel(*loads, *stores, *rest)
        for load in loads:
            load()
        for store in stores:
            store.copy.wait()

    buffers = [
        (pltpu.SMEM if k in scalars else pltpu.VMEM)(a.shape, a.dtype) for k, a in enumerate(args)
    ]
    buffers += [pltpu.VMEM(s.shape, s.dtype) for s in shapes]
    anywhere = pl.BlockSpec(memory_space=pl.ANY)
    return pl.pallas_call(
        body,
        out_shape=shapes,
        in_specs=[anywhere] * n,
        out_specs=[anywhere] * m,
        scratch_shapes=buffers + [pltpu.SemaphoreType.DMA((n + m,))] + list(scratch),
        compiler_params=pltpu.CompilerParams(vmem_limit_bytes=VMEM_LIMIT),
        cost_estimate=pl.CostEstimate(flops=flops, bytes_accessed=size, transcendentals=0),
        name=name,
    )(*args)


def exchange(x):
    return lax.all_to_all(x, "dp", split_axis=0, concat_axis=0, tiled=True)


def on_device(
    text_states, image_states, cot_positive, cot_neg_image, cot_neg_text,
    w_query, w_key, w_value, w_out, ln_gain, neg_image, neg_text, text_feat, image_feat,
):
    me = lax.axis_index("dp").astype(jnp.int32).reshape(1)
    gain = ln_gain.reshape(1, D)
    count = PUSH + PAIRS
    send, feats = call(
        pack_kernel,
        [((DEVS, 16, TILE), BF), ((32, TILE), BF)],
        (neg_image, neg_text, text_feat, image_feat, text_states, cot_neg_image),
        [pltpu.VMEM((16, TILE), F32)],
        name="pack",
        scalars=(0, 1),
    )
    every = lax.all_gather(feats, "dp", axis=0, tiled=True)
    got = exchange(send)
    image_rows = ((PAIRS, LIR, D), BF)
    image_cols = ((PAIRS, D, LIR), BF)
    keys, values, keys_t, values_t, wo_t, wq_t, own_grad, own_ds, own_p, own_q, own_dc = call(
        front_kernel,
        [
            image_rows,
            image_rows,
            image_cols,
            image_cols,
            ((D, D), BF),
            ((D, D), BF),
            ((PAIRS * LT, D), F32),
            ((PAIRS, H * LT, LIR), BF),
            ((PAIRS, H * LT, LIR), BF),
            ((PAIRS * LT, D), BF),
            ((PAIRS * LT, D), BF),
        ],
        (image_states, w_key, w_value, text_states, w_query, w_out, gain, cot_positive),
        [
            pltpu.VMEM((PAIRS, H * LT, LIR), F32),
            pltpu.VMEM((PAIRS * LT, D), BF),
            pltpu.VMEM((PAIRS * LT, D), BF),
            pltpu.VMEM((LIR, D), BF),
        ],
        flops=4 * PAIRS * LIR * D * D + 8 * PAIRS * LT * D * D * 4,
        name="front",
    )
    got, own_grad = lax.optimization_barrier((got, own_grad))
    send, meta, ids = call(
        pick_kernel,
        [((DEVS, 24, TILE), BF), ((8, TILE), jnp.int32), ((DEVS * 8, TILE), BF)],
        (me, got),
        [pltpu.VMEM((DEVS * 8, 2 * TILE), BF)],
        name="pick",
        scalars=(0,),
    )
    got_rows = exchange(send)
    send, q, p, dc, ds = call(
        guest_kernel,
        [
            ((DEVS, 16, TILE), BF),
            ((count * LT, D), BF),
            ((count, H * LT, LIR), BF),
            ((count * LT, D), BF),
            ((count, H * LT, LIR), BF),
        ],
        (
            got_rows, meta, cot_neg_text, w_query, keys_t, values, w_out, gain,
            wo_t, values_t, keys, wq_t,
        ),
        [
            pltpu.VMEM((count, H * LT, LIR), F32),
            pltpu.VMEM((count * LT, D), BF),
            pltpu.VMEM((count * LT, D), BF),
            pltpu.VMEM((count * LT, D), BF),
            pltpu.VMEM((count * LT, D), BF),
            pltpu.VMEM((count * LT, D), F32),
        ],
        flops=8 * count * LT * D * D * 4,
        name="guest",
        scalars=(1,),
    )
    got_back = exchange(send)
    (d_image,) = call(
        image_kernel,
        [((PAIRS, LI, D), BF)],
        (own_ds, own_q, ds, q, own_p, own_dc, p, dc, meta, w_key, w_value),
        [pltpu.VMEM((PAIRS, LIR, D), F32), pltpu.VMEM((PAIRS, LIR, D), F32)],
        flops=8 * PAIRS * LIR * D * D,
        name="image",
        scalars=(8,),
    )
    got_back, d_image = lax.optimization_barrier((got_back, d_image))
    (send,) = call(sum_kernel, [((DEVS, 8, TILE), BF)], (ids, got_back), name="sum")
    send, every = lax.optimization_barrier((send, every))
    got_sum = exchange(send)
    d_text_feat, d_image_feat = call(
        contrast_kernel,
        [((PAIRS, E), F32), ((PAIRS, E), F32)],
        (me, every),
        flops=8 * 512 * 512 * 256,
        name="contrast",
        scalars=(0,),
    )
    got_sum, d_text_feat, d_image_feat = lax.optimization_barrier(
        (got_sum, d_text_feat, d_image_feat)
    )
    (d_text,) = call(join_kernel, [((PAIRS, LT, D), BF)], (own_grad, got_sum), name="join")
    return (d_text, d_image, d_text_feat, d_image_feat)


def solution(mesh):
    return jax.shard_map(
        on_device,
        mesh=mesh,
        in_specs=(
            P("dp", None, None),
            P("dp", None, None),
            P("dp", None, None),
            P("dp", None, None),
            P("dp", None, None),
            P(),
            P(),
            P(),
            P(),
            P(),
            P("dp"),
            P("dp"),
            P("dp", None),
            P("dp", None),
        ),
        out_specs=(P("dp", None, None), P("dp", None, None), P("dp", None), P("dp", None)),
        check_vma=False,
    )
```

```python
import math

import jax
import jax.numpy as jnp
from jax import lax
from jax.experimental import pallas as pl
from jax.experimental.pallas import tpu as pltpu
from jax.sharding import PartitionSpec as P

D = 768
H = 12
E = 256
LT = 16
LI = 197
PAIRS = 4
DEVS = 128
TILE = 128
COLS = D // TILE
PIECES = COLS * LT
LIR = 208
GROUP = 4
GROUPS = H // GROUP
GW = D // GROUPS
GR = GROUP * LT
INV_ROOT = 1.0 / math.sqrt(D // H)
NORM_EPS = 1e-06
SIM_SCALE = 3.0 / math.sqrt(E)
PUSH = 2 * PAIRS
BF = jnp.bfloat16
F32 = jnp.float32
VMEM_LIMIT = 56 * 1024 * 1024

NN = (((1,), (0,)), ((), ()))
NT = (((1,), (1,)), ((), ()))
TN = (((0,), (0,)), ((), ()))


def mm(a, b, dims=NN):
    return lax.dot_general(a, b, dims, preferred_element_type=F32)


def iota(shape, dim):
    return lax.broadcasted_iota(jnp.int32, shape, dim)


def one_hot(mask):
    return jnp.where(mask, 1.0, 0.0).astype(BF)


def pack_kernel(ni_in, nt_in, tf_in, if_in, text_in, cot_in, out):
    out_row = iota((TILE, TILE), 0)
    in_row = iota((TILE, TILE), 1)
    perm = one_hot(in_row == (out_row & 7) * LT + (out_row >> 3))
    row = iota((PAIRS, TILE), 0)
    lane = iota((PAIRS, TILE), 1)
    ni_ref, nt_ref = ni_in(), nt_in()
    ids = jnp.zeros((PAIRS, TILE), jnp.int32)
    for a in range(PAIRS):
        ni = ni_ref[a]
        nt = nt_ref[a]
        for j, val in enumerate((ni >> 2, ni & 3, nt >> 2, nt & 3)):
            ids = jnp.where(jnp.logical_and(row == a, lane == j), val, ids)
    ids = ids.astype(F32)
    tf = tf_in()[:, :TILE].astype(F32)
    im = if_in()[:, :TILE].astype(F32)
    even = jnp.concatenate([ids, tf], axis=0)
    odd = jnp.concatenate([ids, im], axis=0)
    shared = jnp.where(iota((LT, 8, TILE), 0) % 2 == 0, even[None], odd[None])
    rows = jnp.concatenate([text_in()[...], cot_in()[...]], axis=0).reshape(TILE, D)
    pieces = mm(perm, rows)
    for c in range(COLS):
        part = pieces[:, c * TILE : (c + 1) * TILE].reshape(LT, 8, TILE)
        out.ref[c * LT : (c + 1) * LT] = jnp.concatenate([shared, part], axis=1).astype(BF)
    for c in range(COLS, DEVS // LT):
        out.ref[c * LT : (c + 1) * LT] = jnp.concatenate(
            [shared, jnp.zeros((LT, 8, TILE), F32)], axis=1
        ).astype(BF)
    out.send()


def pick_kernel(got_in, tf_in, if_in, me_in, out, meta_out, ids_out, pair_tab):
    total = DEVS * PAIRS
    got = got_in()[...].astype(F32)
    ids = got[:, :4].reshape(total, TILE)
    pair_tab[:, :TILE] = got[:, 8:12].reshape(total, TILE).astype(BF)
    pair_tab[:, TILE:] = got[:, 12:].reshape(total, TILE).astype(BF)
    owner_col = ids[:, 0:1]
    target_col = ids[:, 2:3] * PAIRS + ids[:, 3:4]
    eye = one_hot(iota((8, TILE), 0) == iota((8, TILE), 1))
    flat = mm(eye, ids.astype(BF), NT)
    owner_row = flat[0:1]
    local_row = flat[1:2]
    step = 128
    ranks = []
    for b in range(total // step):
        earlier = iota((step, total), 1) < iota((step, total), 0) + b * step
        same = owner_col[b * step : (b + 1) * step] == owner_row
        ranks.append(
            jnp.sum(jnp.where(jnp.logical_and(same, earlier), 1.0, 0.0), axis=1, keepdims=True)
        )
    rank_col = jnp.concatenate(ranks, axis=0)
    with_rank = jnp.where(iota((total, TILE), 1) == 4, rank_col, ids).astype(BF)
    ids_out.ref[...] = with_rank
    ids_out.send()
    flat_rank = mm(one_hot(iota((8, TILE), 1) == 4), with_rank, NT)[0:1]
    key_row = owner_row * PUSH + flat_rank
    slot_col = iota((DEVS * PUSH, 1), 0).astype(F32)
    pair_row = iota((1, total), 1).astype(F32)
    tf = tf_in()[:, TILE:].astype(F32)
    im = if_in()[:, TILE:].astype(F32)
    devs = 32
    feats = jnp.where(iota((devs, PAIRS, TILE), 0) % 2 == 0, tf[None], im[None])
    for b in range(DEVS // devs):
        slots = slice(b * devs * PUSH, (b + 1) * devs * PUSH)
        pairs = slice(b * devs * PAIRS, (b + 1) * devs * PAIRS)
        pushed = mm(one_hot(slot_col[slots] == key_row), pair_tab[...])
        pulled = mm(one_hot(target_col[pairs] == pair_row), pair_tab[:, :TILE])
        out.ref[b * devs : (b + 1) * devs] = jnp.concatenate(
            [
                pushed[:, :TILE].reshape(devs, PUSH, TILE),
                pushed[:, TILE:].reshape(devs, PUSH, TILE),
                jnp.concatenate([pulled.reshape(devs, PAIRS, TILE), feats], axis=1),
            ],
            axis=1,
        ).astype(BF)
    out.send()
    mine = (iota((PUSH, total), 0) + PUSH * me_in()[0]).astype(F32) == key_row
    live = jnp.sum(jnp.where(mine, 1.0, 0.0), axis=1, keepdims=True)
    target = jnp.sum(jnp.where(mine, local_row, 0.0), axis=1, keepdims=True)
    meta = jnp.where(live > 0, target, -1.0).astype(jnp.int32)
    meta_out.ref[...] = jnp.broadcast_to(meta, (PUSH, TILE))
    meta_out.send()


def sum_kernel(ids_in, got_in, out):
    total = DEVS * PAIRS
    ids_ref = ids_in()
    ids = ids_ref[...].astype(F32)
    key_col = ids[:, 0:1] * PUSH + ids[:, 4:5]
    eye = one_hot(iota((8, TILE), 0) == iota((8, TILE), 1))
    flat = mm(eye, ids_ref[...], NT)
    target_row = flat[2:3] * PAIRS + flat[3:4]
    pair_col = iota((total, 1), 0).astype(F32)
    slot_row = iota((1, DEVS * PUSH), 1).astype(F32)
    got = got_in()[...].astype(F32)
    push = got[:, :PUSH].reshape(DEVS * PUSH, TILE).astype(BF)
    pull = got[:, PUSH : PUSH + PAIRS].reshape(total, TILE).astype(BF)
    devs = 32
    for b in range(DEVS // devs):
        block = slice(b * devs * PAIRS, (b + 1) * devs * PAIRS)
        both = mm(one_hot(key_col[block] == slot_row), push)
        both += mm(one_hot(pair_col[block] == target_row), pull)
        out.ref[b * devs : (b + 1) * devs] = jnp.concatenate(
            [both.reshape(devs, PAIRS, TILE), jnp.zeros((devs, PAIRS, TILE), F32)], axis=1
        ).astype(BF)
    out.send()


def feats_kernel(first_in, second_in, out):
    total = DEVS * PAIRS
    first = first_in()[:, 0:8].astype(F32)[:, 4:]
    out.ref[:, :TILE] = first.reshape(total, TILE).astype(BF)
    second = second_in()[:, 16:24].astype(F32)[:, 4:]
    out.ref[:, TILE:] = second.reshape(total, TILE).astype(BF)
    out.send()


def join_kernel(own_in, got_in, out):
    parts = []
    got_ref = got_in()
    for c in range(COLS):
        got = got_ref[c * LT : (c + 1) * LT].astype(F32)
        parts.append(got.reshape(TILE, TILE).astype(BF))
    pieces = jnp.concatenate(parts, axis=1)
    out_row = iota((PAIRS * LT, TILE), 0)
    in_row = iota((PAIRS * LT, TILE), 1)
    perm = one_hot(in_row == (out_row & 15) * 8 + (out_row >> 4))
    total = own_in()[...] + mm(perm, pieces)
    out.ref[...] = total.astype(BF).reshape(PAIRS, LT, D)
    out.send()


def head_mask():
    return one_hot((iota((GR, GW), 0) >> 4) == (iota((GR, GW), 1) >> 6))


def spread(rows, mask):
    return jnp.concatenate([rows] * GROUP, axis=0) * mask


def fold(full):
    head = iota((LT, GW), 1) >> 6
    out = full[0:LT]
    for h in range(1, GROUP):
        out = jnp.where(head == h, full[h * LT : (h + 1) * LT], out)
    return out


def parts_of(items, targets):
    for i, target in zip(items, targets):
        at = pl.ds(pl.multiple_of(i * LT, LT), LT)
        for g in range(GROUPS):
            yield i, target, at, slice(g * GW, (g + 1) * GW), slice(g * GR, (g + 1) * GR)


def attend(items, targets, keys_t, values, query, weights, probs, context):
    mask = head_mask()
    lane = iota((GR, LIR), 1)
    work = list(parts_of(items, targets))
    scores = []
    for i, target, at, cols, rows in work:
        s = mm(spread(query[at, cols], mask), keys_t[target, cols, :]) * INV_ROOT
        scores.append(jnp.where(lane < LI, s, -1e30))
    halves = []
    for (i, target, at, cols, rows), s in zip(work, scores):
        w = jnp.exp(s - jnp.max(s, axis=1, keepdims=True))
        w = w / jnp.sum(w, axis=1, keepdims=True)
        half = w.astype(BF)
        weights[i, rows, :] = w
        probs[i, rows, :] = half
        halves.append(half)
    for (i, target, at, cols, rows), half in zip(work, halves):
        context[at, cols] = fold(mm(half, values[target, :, cols])).astype(BF)


def attend_back(items, targets, keys, values_t, d_context, weights, d_scores, d_query):
    mask = head_mask()
    work = list(parts_of(items, targets))
    d_probs = []
    for i, target, at, cols, rows in work:
        d_probs.append(mm(spread(d_context[at, cols], mask), values_t[target, cols, :]))
    halves = []
    for (i, target, at, cols, rows), dp in zip(work, d_probs):
        w = weights[i, rows, :]
        ds = w * (dp - jnp.sum(w * dp, axis=1, keepdims=True)) * INV_ROOT
        ds = ds.astype(BF)
        d_scores[i, rows, :] = ds
        halves.append(ds)
    for (i, target, at, cols, rows), ds in zip(work, halves):
        d_query[at, cols] = fold(mm(ds, keys[target, :, cols])).astype(BF)


def norm_back(summed, cot, gain):
    centred = summed - jnp.mean(summed, axis=1, keepdims=True)
    inv_sigma = lax.rsqrt(jnp.mean(centred * centred, axis=1, keepdims=True) + NORM_EPS)
    normed = centred * inv_sigma
    gz = cot * gain
    return inv_sigma * (
        gz
        - jnp.mean(gz, axis=1, keepdims=True)
        - normed * jnp.mean(gz * normed, axis=1, keepdims=True)
    )


def project_kernel(
    image_in, wk_in, wv_in, wo_in, wq_in,
    keys_o, values_o, keys_t_o, values_t_o, wo_t_o, wq_t_o,
    padded,
):
    image = image_in()
    padded[...] = jnp.zeros_like(padded)
    for t in range(PAIRS):
        padded[0:LI] = image[t]
        rows = padded[...]
        for w_in, plain, turned in ((wk_in, keys_o, keys_t_o), (wv_in, values_o, values_t_o)):
            made = mm(rows, w_in()[...]).astype(BF)
            plain.ref[t] = made
            turned.ref[t] = made.T
    for o in (keys_o, values_o, keys_t_o, values_t_o):
        o.send()
    wo_t_o.ref[...] = wo_in()[...].T
    wo_t_o.send()
    wq_t_o.ref[...] = wq_in()[...].T
    wq_t_o.send()


def own_kernel(
    text_in, wq_in, keys_t_in, values_in, wo_in, gain_in, cot_in,
    wo_t_in, values_t_in, keys_in, wq_t_in,
    grad_o, d_scores, probs, query, d_context,
    weights, context, d_query,
):
    texts = text_in()[...].reshape(PAIRS * LT, D)
    query.ref[...] = mm(texts, wq_in()[...]).astype(BF)
    query.send()
    every = list(range(PAIRS))
    attend(every, every, keys_t_in(), values_in(), query.ref, weights, probs.ref, context)
    probs.send()
    summed = mm(context[...], wo_in()[...]) + texts.astype(F32)
    cots = cot_in()[...].reshape(PAIRS * LT, D).astype(F32)
    d_summed = norm_back(summed, cots, gain_in()[...])
    d_context.ref[...] = mm(d_summed.astype(BF), wo_t_in()[...]).astype(BF)
    d_context.send()
    attend_back(
        every, every, keys_in(), values_t_in(), d_context.ref, weights, d_scores.ref, d_query
    )
    d_scores.send()
    grad_o.ref[...] = d_summed + mm(d_query[...], wq_t_in()[...])
    grad_o.send()


def guest_kernel(
    got_in, meta_in, cot_in, wq_in, keys_t_in, values_in, wo_in, gain_in,
    wo_t_in, values_t_in, keys_in, wq_t_in,
    out, query, probs, d_context, d_scores,
    weights, context, d_query, texts, cots, d_summed_ref,
):
    count = PUSH + PAIRS
    out_row = iota((20 * LT, 24 * LT), 0)
    in_row = iota((20 * LT, 24 * LT), 1)
    perm = one_hot(in_row == (out_row & 15) * 24 + (out_row >> 4))
    got_ref = got_in()
    parts = []
    for c in range(COLS):
        got = got_ref[c * LT : (c + 1) * LT].astype(F32)
        parts.append(got.reshape(LT * 24, TILE).astype(BF))
    pieces = jnp.concatenate(parts, axis=1)
    rows = mm(perm, pieces)
    push_rows = PUSH * LT
    texts[:push_rows] = rows[:push_rows].astype(BF)
    texts[push_rows:] = rows[2 * push_rows :].astype(BF)
    cots[:push_rows] = rows[push_rows : 2 * push_rows].astype(BF)
    cots[push_rows:] = cot_in()[...].reshape(PAIRS * LT, D)
    query.ref[...] = mm(texts[...], wq_in()[...]).astype(BF)
    query.send()
    meta = meta_in()
    own = list(range(PAIRS))
    pulled = [PUSH + j for j in own]
    keys_t, values = keys_t_in(), values_in()

    def batch(s):
        items = [s * PAIRS + u for u in range(PAIRS)]
        return items, [jnp.maximum(meta[i, 0], 0) for i in items]

    def forward(s, carry):
        attend(*batch(s), keys_t, values, query.ref, weights, probs.ref, context)
        return carry

    lax.fori_loop(0, PUSH // PAIRS, forward, 0)
    attend(pulled, own, keys_t, values, query.ref, weights, probs.ref, context)
    probs.send()
    summed = mm(context[...], wo_in()[...]) + texts[...].astype(F32)
    d_summed = norm_back(summed, cots[...].astype(F32), gain_in()[...])
    d_summed_ref[...] = d_summed
    d_context.ref[...] = mm(d_summed.astype(BF), wo_t_in()[...]).astype(BF)
    d_context.send()
    keys, values_t = keys_in(), values_t_in()

    def backward(s, carry):
        attend_back(*batch(s), keys, values_t, d_context.ref, weights, d_scores.ref, d_query)
        return carry

    lax.fori_loop(0, PUSH // PAIRS, backward, 0)
    attend_back(pulled, own, keys, values_t, d_context.ref, weights, d_scores.ref, d_query)
    d_scores.send()
    grads = (d_summed_ref[...] + mm(d_query[...], wq_t_in()[...])).astype(BF)
    out_row = iota((LT * 16, count * LT), 0)
    in_row = iota((LT * 16, count * LT), 1)
    perm = one_hot(in_row == (out_row & 15) * LT + (out_row >> 4))
    back = mm(perm, grads).astype(BF)
    for c in range(COLS):
        out.ref[c * LT : (c + 1) * LT] = back[:, c * TILE : (c + 1) * TILE].reshape(LT, 16, TILE)
    out.ref[PIECES:] = jnp.zeros((DEVS - PIECES, 16, TILE), BF)
    out.send()


def image_kernel(
    own_ds_in, own_q_in, ds_in, q_in, own_p_in, own_dc_in, p_in, dc_in, meta_in, wk_in, wv_in,
    out, d_keys, d_values,
):
    mask = head_mask()

    def term(scores, rows):
        return mm(scores, rows, TN)

    sides = (
        (d_keys, own_ds_in(), own_q_in(), ds_in(), q_in()),
        (d_values, own_p_in(), own_dc_in(), p_in(), dc_in()),
    )
    for t in range(PAIRS):
        at = slice(t * LT, (t + 1) * LT)
        pat = slice((PUSH + t) * LT, (PUSH + t + 1) * LT)
        for g in range(GROUPS):
            cols = slice(g * GW, (g + 1) * GW)
            rows = slice(g * GR, (g + 1) * GR)
            for total, own_left, own_right, left, right in sides:
                total[t, :, cols] = term(
                    jnp.concatenate([own_left[t, rows, :], left[PUSH + t, rows, :]], axis=0),
                    jnp.concatenate(
                        [spread(own_right[at, cols], mask), spread(right[pat, cols], mask)], axis=0
                    ),
                )
    meta = meta_in()

    def visit(i, carry):
        target = meta[i, 0]

        @pl.when(target >= 0)
        def _():
            at = pl.ds(pl.multiple_of(i * LT, LT), LT)
            for g in range(GROUPS):
                cols = slice(g * GW, (g + 1) * GW)
                rows = slice(g * GR, (g + 1) * GR)
                for total, _, _, left, right in sides:
                    total[target, :, cols] += term(left[i, rows, :], spread(right[at, cols], mask))

        return carry

    lax.fori_loop(0, PUSH, visit, 0)
    wk, wv = wk_in()[...].T, wv_in()[...].T
    for t in range(PAIRS):
        total = mm(d_keys[t].astype(BF), wk) + mm(d_values[t].astype(BF), wv)
        out.ref[t] = total.astype(BF)[:LI]
    out.send()


def log_sums(table):
    peak = jnp.max(table, axis=0, keepdims=True)
    return peak + jnp.log(jnp.sum(jnp.exp(table - peak), axis=0, keepdims=True))


def contrast_kernel(mine_in, other_in, tf_in, if_in, me_in, d_text_o, d_image_o):
    total = DEVS * PAIRS
    me = me_in()[0]
    mine, other = mine_in()[...], other_in()[...]
    even = (me & 1) == 0
    texts = jnp.where(even, mine, other)
    images = jnp.where(even, other, mine)
    texts_t, images_t = texts.T, images.T
    row_lse = log_sums(mm(images, texts_t) * SIM_SCALE)
    col_lse = log_sums(mm(texts, images_t) * SIM_SCALE)
    own = iota((PAIRS, total), 0) + me * PAIRS == iota((PAIRS, total), 1)

    def side(rows_in, turned, plain, across_lse, o):
        similar = mm(rows_in()[...], turned) * SIM_SCALE
        peak = jnp.max(similar, axis=1, keepdims=True)
        own_lse = peak + jnp.log(jnp.sum(jnp.exp(similar - peak), axis=1, keepdims=True))
        d_similar = 0.5 * jnp.exp(similar - own_lse) + 0.5 * jnp.exp(similar - across_lse)
        d_similar = d_similar - jnp.where(own, 1.0, 0.0)
        high = d_similar.astype(BF)
        rest = d_similar - high.astype(F32)
        middle = rest.astype(BF)
        low = (rest - middle.astype(F32)).astype(BF)
        o.ref[...] = SIM_SCALE * (mm(high, plain) + (mm(middle, plain) + mm(low, plain)))
        o.send()

    side(tf_in, images_t, images, col_lse, d_text_o)
    side(if_in, texts_t, texts, row_lse, d_image_o)


class Loaded:
    def __init__(self, src, dst, sem):
        self.copy = pltpu.make_async_copy(src, dst, sem)
        self.copy.start()
        self.buffer = dst
        self.waited = False

    def __call__(self):
        if not self.waited:
            self.copy.wait()
            self.waited = True
        return self.buffer


class Stored:
    def __init__(self, ref, dst, sem):
        self.ref = ref
        self.copy = pltpu.make_async_copy(ref, dst, sem)

    def send(self):
        self.copy.start()


def call(kernel, outs, args, scratch=(), flops=0, name=None, scalars=()):
    shapes = [jax.ShapeDtypeStruct(s, d) for s, d in outs]
    n, m = len(args), len(outs)
    size = sum(a.size * a.dtype.itemsize for a in args)
    size += sum(math.prod(s.shape) * s.dtype.itemsize for s in shapes)

    def body(*refs):
        arrays, buffers = refs[: n + m], refs[n + m : 2 * (n + m)]
        sems, rest = refs[2 * (n + m)], refs[2 * (n + m) + 1 :]
        loads = [Loaded(arrays[k], buffers[k], sems.at[k]) for k in range(n)]
        stores = [Stored(buffers[k], arrays[k], sems.at[k]) for k in range(n, n + m)]
        kernel(*loads, *stores, *rest)
        for load in loads:
            load()
        for store in stores:
            store.copy.wait()

    buffers = [
        (pltpu.SMEM if k in scalars else pltpu.VMEM)(a.shape, a.dtype) for k, a in enumerate(args)
    ]
    buffers += [pltpu.VMEM(s.shape, s.dtype) for s in shapes]
    anywhere = pl.BlockSpec(memory_space=pltpu.HBM)
    return pl.pallas_call(
        body,
        out_shape=shapes,
        in_specs=[anywhere] * n,
        out_specs=[anywhere] * m,
        scratch_shapes=buffers + [pltpu.SemaphoreType.DMA((n + m,))] + list(scratch),
        compiler_params=pltpu.CompilerParams(vmem_limit_bytes=VMEM_LIMIT),
        cost_estimate=pl.CostEstimate(flops=flops, bytes_accessed=size, transcendentals=0),
        name=name,
    )(*args)


def exchange(x):
    return lax.all_to_all(x, "dp", split_axis=0, concat_axis=0, tiled=True)


def on_device(
    text_states, image_states, cot_positive, cot_neg_image, cot_neg_text,
    w_query, w_key, w_value, w_out, ln_gain, neg_image, neg_text, text_feat, image_feat,
):
    me = lax.axis_index("dp").astype(jnp.int32).reshape(1)
    gain = ln_gain.reshape(1, D)
    count = PUSH + PAIRS
    (send,) = call(
        pack_kernel,
        [((DEVS, 16, TILE), BF)],
        (neg_image, neg_text, text_feat, image_feat, text_states, cot_neg_image),
        name="pack",
        scalars=(0, 1),
    )
    got = exchange(send)
    image_rows = ((PAIRS, LIR, D), BF)
    image_cols = ((PAIRS, D, LIR), BF)
    keys, values, keys_t, values_t, wo_t, wq_t = call(
        project_kernel,
        [image_rows, image_rows, image_cols, image_cols, ((D, D), BF), ((D, D), BF)],
        (image_states, w_key, w_value, w_out, w_query),
        [pltpu.VMEM((LIR, D), BF)],
        flops=4 * PAIRS * LIR * D * D,
        name="project",
    )
    got, keys = lax.optimization_barrier((got, keys))
    send, meta, ids = call(
        pick_kernel,
        [((DEVS, 24, TILE), BF), ((PUSH, TILE), jnp.int32), ((DEVS * PAIRS, TILE), BF)],
        (got, text_feat, image_feat, me),
        [pltpu.VMEM((DEVS * PAIRS, 2 * TILE), BF)],
        name="pick",
        scalars=(3,),
    )
    send, keys = lax.optimization_barrier((send, keys))
    got_rows = exchange(send)
    own_grad, own_ds, own_p, own_q, own_dc = call(
        own_kernel,
        [
            ((PAIRS * LT, D), F32),
            ((PAIRS, H * LT, LIR), BF),
            ((PAIRS, H * LT, LIR), BF),
            ((PAIRS * LT, D), BF),
            ((PAIRS * LT, D), BF),
        ],
        (
            text_states, w_query, keys_t, values, w_out, gain, cot_positive,
            wo_t, values_t, keys, wq_t,
        ),
        [
            pltpu.VMEM((PAIRS, H * LT, LIR), F32),
            pltpu.VMEM((PAIRS * LT, D), BF),
            pltpu.VMEM((PAIRS * LT, D), BF),
        ],
        flops=8 * PAIRS * LT * D * D * 4,
        name="own",
    )
    got_rows, own_grad = lax.optimization_barrier((got_rows, own_grad))
    send, q, p, dc, ds = call(
        guest_kernel,
        [
            ((DEVS, 16, TILE), BF),
            ((count * LT, D), BF),
            ((count, H * LT, LIR), BF),
            ((count * LT, D), BF),
            ((count, H * LT, LIR), BF),
        ],
        (
            got_rows, meta, cot_neg_text, w_query, keys_t, values, w_out, gain,
            wo_t, values_t, keys, wq_t,
        ),
        [
            pltpu.VMEM((count, H * LT, LIR), F32),
            pltpu.VMEM((count * LT, D), BF),
            pltpu.VMEM((count * LT, D), BF),
            pltpu.VMEM((count * LT, D), BF),
            pltpu.VMEM((count * LT, D), BF),
            pltpu.VMEM((count * LT, D), F32),
        ],
        flops=8 * count * LT * D * D * 4,
        name="guest",
        scalars=(1,),
    )
    send, got, got_rows = lax.optimization_barrier((send, got, got_rows))
    got_back = exchange(send)
    (feats,) = call(
        feats_kernel, [((DEVS * PAIRS, E), BF)], (got, got_rows), name="feats"
    )
    swapped = lax.ppermute(feats, "dp", [(i, i ^ 1) for i in range(DEVS)])
    feats, ds = lax.optimization_barrier((feats, ds))
    (d_image,) = call(
        image_kernel,
        [((PAIRS, LI, D), BF)],
        (own_ds, own_q, ds, q, own_p, own_dc, p, dc, meta, w_key, w_value),
        [pltpu.VMEM((PAIRS, LIR, D), F32), pltpu.VMEM((PAIRS, LIR, D), F32)],
        flops=8 * PAIRS * LIR * D * D,
        name="image",
        scalars=(8,),
    )
    got_back, d_image, swapped = lax.optimization_barrier((got_back, d_image, swapped))
    (send,) = call(sum_kernel, [((DEVS, 8, TILE), BF)], (ids, got_back), name="sum")
    send, swapped = lax.optimization_barrier((send, swapped))
    got_sum = exchange(send)
    d_text_feat, d_image_feat = call(
        contrast_kernel,
        [((PAIRS, E), F32), ((PAIRS, E), F32)],
        (feats, swapped, text_feat, image_feat, me),
        flops=8 * 512 * 512 * 256,
        name="contrast",
        scalars=(4,),
    )
    got_sum, d_text_feat, d_image_feat = lax.optimization_barrier(
        (got_sum, d_text_feat, d_image_feat)
    )
    (d_text,) = call(join_kernel, [((PAIRS, LT, D), BF)], (own_grad, got_sum), name="join")
    return (d_text, d_image, d_text_feat, d_image_feat)


def solution(mesh):
    return jax.shard_map(
        on_device,
        mesh=mesh,
        in_specs=(
            P("dp", None, None),
            P("dp", None, None),
            P("dp", None, None),
            P("dp", None, None),
            P("dp", None, None),
            P(),
            P(),
            P(),
            P(),
            P(),
            P("dp"),
            P("dp"),
            P("dp", None),
            P("dp", None),
        ),
        out_specs=(P("dp", None, None), P("dp", None, None), P("dp", None), P("dp", None)),
        check_vma=False,
    )
```

```python
import math

import jax
import jax.numpy as jnp
from jax import lax
from jax.experimental import pallas as pl
from jax.experimental.pallas import tpu as pltpu
from jax.sharding import PartitionSpec as P

D = 768
H = 12
E = 256
LT = 16
LI = 197
PAIRS = 4
DEVS = 128
TILE = 128
COLS = D // TILE
PIECES = COLS * LT
LIR = 208
GROUP = 4
GROUPS = H // GROUP
GW = D // GROUPS
GR = GROUP * LT
INV_ROOT = 1.0 / math.sqrt(D // H)
NORM_EPS = 1e-06
SIM_SCALE = 3.0 / math.sqrt(E)
PUSH = 2 * PAIRS
BF = jnp.bfloat16
F32 = jnp.float32
MIB = 1024 * 1024
SEND_PARTS = 8

NN = (((1,), (0,)), ((), ()))
NT = (((1,), (1,)), ((), ()))
TN = (((0,), (0,)), ((), ()))


def mm(a, b, dims=NN):
    return lax.dot_general(a, b, dims, preferred_element_type=F32)


def iota(shape, dim):
    return lax.broadcasted_iota(jnp.int32, shape, dim)


def one_hot(mask):
    return jnp.where(mask, 1.0, 0.0).astype(BF)


def pack_kernel(ni_in, nt_in, tf_in, if_in, text_in, cot_in, out):
    out_row = iota((TILE, TILE), 0)
    in_row = iota((TILE, TILE), 1)
    perm = one_hot(in_row == (out_row & 7) * LT + (out_row >> 3))
    row = iota((PAIRS, TILE), 0)
    lane = iota((PAIRS, TILE), 1)
    ni_ref, nt_ref = ni_in(), nt_in()
    ids = jnp.zeros((PAIRS, TILE), jnp.int32)
    for a in range(PAIRS):
        ni = ni_ref[a]
        nt = nt_ref[a]
        for j, val in enumerate((ni >> 2, ni & 3, nt >> 2, nt & 3)):
            ids = jnp.where(jnp.logical_and(row == a, lane == j), val, ids)
    ids = ids.astype(F32)
    tf = tf_in()[:, :TILE].astype(F32)
    im = if_in()[:, :TILE].astype(F32)
    even = jnp.concatenate([ids, tf], axis=0)
    odd = jnp.concatenate([ids, im], axis=0)
    shared = jnp.where(iota((LT, 8, TILE), 0) % 2 == 0, even[None], odd[None])
    rows = jnp.concatenate([text_in()[...], cot_in()[...]], axis=0).reshape(TILE, D)
    pieces = mm(perm, rows)
    for c in range(COLS):
        part = pieces[:, c * TILE : (c + 1) * TILE].reshape(LT, 8, TILE)
        out.ref[c * LT : (c + 1) * LT] = jnp.concatenate([shared, part], axis=1).astype(BF)
        out.send(c * LT, (c + 1) * LT)
    blank = jnp.concatenate([shared, jnp.zeros((LT, 8, TILE), F32)], axis=1).astype(BF)
    for c in range(COLS, DEVS // LT):
        out.ref[c * LT : (c + 1) * LT] = blank
    out.send(PIECES, DEVS)


def column_to_row(rows, *lanes):
    pick = jnp.zeros((8, TILE), BF)
    for k, lane in enumerate(lanes):
        here = jnp.logical_and(iota((8, TILE), 0) == k, iota((8, TILE), 1) == lane)
        pick = pick + one_hot(here)
    return mm(pick, rows, NT)


def rank_pairs(ids):
    total = DEVS * PAIRS
    owner_col = ids[:, 0:1]
    owner_row = column_to_row(ids.astype(BF), 0)[0:1]
    step = 128
    ranks = []
    for b in range(total // step):
        earlier = iota((step, total), 1) < iota((step, total), 0) + b * step
        same = owner_col[b * step : (b + 1) * step] == owner_row
        ranks.append(
            jnp.sum(jnp.where(jnp.logical_and(same, earlier), 1.0, 0.0), axis=1, keepdims=True)
        )
    rank_col = jnp.concatenate(ranks, axis=0)
    with_rank = jnp.where(iota((total, TILE), 1) == 4, rank_col, ids).astype(BF)
    flat = column_to_row(with_rank, 0, 1, 4)
    return with_rank, flat[0:1] * PUSH + flat[2:3], flat[1:2]


def pick_kernel(got_in, tf_in, if_in, out, ids_out, pair_tab):
    total = DEVS * PAIRS
    got = got_in()[...].astype(F32)
    ids = got[:, :4].reshape(total, TILE)
    pair_tab[:, :TILE] = got[:, 8:12].reshape(total, TILE).astype(BF)
    pair_tab[:, TILE:] = got[:, 12:].reshape(total, TILE).astype(BF)
    target_col = ids[:, 2:3] * PAIRS + ids[:, 3:4]
    with_rank, key_row, _ = rank_pairs(ids)
    ids_out.ref[...] = with_rank
    ids_out.send()
    slot_col = iota((DEVS * PUSH, 1), 0).astype(F32)
    pair_row = iota((1, total), 1).astype(F32)
    tf = tf_in()[:, TILE:].astype(F32)
    im = if_in()[:, TILE:].astype(F32)
    devs = 32
    feats = jnp.where(iota((devs, PAIRS, TILE), 0) % 2 == 0, tf[None], im[None])
    for b in range(DEVS // devs):
        slots = slice(b * devs * PUSH, (b + 1) * devs * PUSH)
        pairs = slice(b * devs * PAIRS, (b + 1) * devs * PAIRS)
        pushed = mm(one_hot(slot_col[slots] == key_row), pair_tab[...])
        pulled = mm(one_hot(target_col[pairs] == pair_row), pair_tab[:, :TILE])
        out.ref[b * devs : (b + 1) * devs] = jnp.concatenate(
            [
                pushed[:, :TILE].reshape(devs, PUSH, TILE),
                pushed[:, TILE:].reshape(devs, PUSH, TILE),
                jnp.concatenate([pulled.reshape(devs, PAIRS, TILE), feats], axis=1),
            ],
            axis=1,
        ).astype(BF)
        out.send(b * devs, (b + 1) * devs)


def sum_kernel(ids_in, got_in, out):
    total = DEVS * PAIRS
    ids_ref = ids_in()
    ids = ids_ref[...].astype(F32)
    key_col = ids[:, 0:1] * PUSH + ids[:, 4:5]
    flat = column_to_row(ids_ref[...], 2, 3)
    target_row = flat[0:1] * PAIRS + flat[1:2]
    pair_col = iota((total, 1), 0).astype(F32)
    slot_row = iota((1, DEVS * PUSH), 1).astype(F32)
    got = got_in()[...].astype(F32).reshape(DEVS, PUSH + PAIRS, TILE)
    push = got[:, :PUSH].reshape(DEVS * PUSH, TILE).astype(BF)
    pull = got[:, PUSH:].reshape(total, TILE).astype(BF)
    devs = 32
    for b in range(DEVS // devs):
        block = slice(b * devs * PAIRS, (b + 1) * devs * PAIRS)
        both = mm(one_hot(key_col[block] == slot_row), push)
        both += mm(one_hot(pair_col[block] == target_row), pull)
        out.ref[b * devs : (b + 1) * devs] = both.reshape(devs, PAIRS, TILE).astype(BF)
        out.send(b * devs, (b + 1) * devs)


def join_kernel(own_in, got_in, out):
    parts = []
    got_ref = got_in()
    for c in range(COLS):
        got = got_ref[c * LT : (c + 1) * LT].astype(F32)
        parts.append(got.reshape(LT * PAIRS, TILE).astype(BF))
    pieces = jnp.concatenate(parts, axis=1)
    out_row = iota((PAIRS * LT, LT * PAIRS), 0)
    in_row = iota((PAIRS * LT, LT * PAIRS), 1)
    perm = one_hot(in_row == (out_row & 15) * PAIRS + (out_row >> 4))
    total = own_in()[...] + mm(perm, pieces)
    out.ref[...] = total.astype(BF).reshape(PAIRS, LT, D)
    out.send()


def head_mask(scale=1.0):
    same = (iota((GR, GW), 0) >> 4) == (iota((GR, GW), 1) >> 6)
    return jnp.where(same, scale, 0.0).astype(BF)


def spread(rows, mask):
    return jnp.concatenate([rows] * GROUP, axis=0) * mask


def fold(full):
    head = iota((LT, GW), 1) >> 6
    out = full[0:LT]
    for h in range(1, GROUP):
        out = jnp.where(head == h, full[h * LT : (h + 1) * LT], out)
    return out


def parts_of(items, targets):
    for i, target in zip(items, targets):
        at = slice(i * LT, (i + 1) * LT)
        for g in range(GROUPS):
            yield i, target, at, slice(g * GW, (g + 1) * GW), slice(g * GR, (g + 1) * GR)


def attend(items, targets, keys_t, values, query, weights, probs, context):
    mask = head_mask(INV_ROOT)
    lane = iota((GR, LIR), 1)
    work = list(parts_of(items, targets))
    scores = []
    for i, target, at, cols, rows in work:
        s = mm(spread(query[at, cols], mask), keys_t[target, cols, :])
        scores.append(jnp.where(lane < LI, s, -1e30))
    halves = []
    for (i, target, at, cols, rows), s in zip(work, scores):
        w = jnp.exp(s - jnp.max(s, axis=1, keepdims=True))
        w = w * (1.0 / jnp.sum(w, axis=1, keepdims=True))
        half = w.astype(BF)
        weights[i, rows, :] = w
        probs[i, rows, :] = half
        halves.append(half)
    for (i, target, at, cols, rows), half in zip(work, halves):
        context[at, cols] = fold(mm(half, values[target, :, cols])).astype(BF)


def attend_back(items, targets, keys, values_t, d_context, weights, d_scores, d_query):
    mask = head_mask(INV_ROOT)
    work = list(parts_of(items, targets))
    d_probs = []
    for i, target, at, cols, rows in work:
        d_probs.append(mm(spread(d_context[at, cols], mask), values_t[target, cols, :]))
    halves = []
    for (i, target, at, cols, rows), dp in zip(work, d_probs):
        w = weights[i, rows, :]
        ds = w * (dp - jnp.sum(w * dp, axis=1, keepdims=True))
        ds = ds.astype(BF)
        d_scores[i, rows, :] = ds
        halves.append(ds)
    for (i, target, at, cols, rows), ds in zip(work, halves):
        d_query[at, cols] = fold(mm(ds, keys[target, :, cols])).astype(BF)


def norm_back(summed, cot, gain):
    centred = summed - jnp.mean(summed, axis=1, keepdims=True)
    inv_sigma = lax.rsqrt(jnp.mean(centred * centred, axis=1, keepdims=True) + NORM_EPS)
    normed = centred * inv_sigma
    gz = cot * gain
    return inv_sigma * (
        gz
        - jnp.mean(gz, axis=1, keepdims=True)
        - normed * jnp.mean(gz * normed, axis=1, keepdims=True)
    )


def project_kernel(image_in, wk_in, wv_in, keys_o, values_o, keys_t_o, values_t_o, padded):
    image = image_in()
    padded[...] = jnp.zeros_like(padded)
    for t in range(PAIRS):
        padded[t * LIR : t * LIR + LI] = image[t]
    for w_in, plain, turned in ((wk_in, keys_o, keys_t_o), (wv_in, values_o, values_t_o)):
        w = w_in()
        for g in range(GROUPS):
            cols = slice(g * GW, (g + 1) * GW)
            made = mm(padded[...], w[:, cols]).astype(BF)
            for t in range(PAIRS):
                rows = made[t * LIR : (t + 1) * LIR]
                plain.ref[t, :, cols] = rows
                turned.ref[t, cols, :] = rows.T
        plain.send()
        turned.send()


def own_kernel(
    text_in, wq_in, keys_t_in, values_in, wo_in, gain_in, cot_in, values_t_in, keys_in,
    me_in, got_in, wk_in, wv_in,
    grad_o, d_scores, probs, query, d_context, wo_t_o, wq_t_o, wk_t_o, wv_t_o, meta_o, feats_o,
    weights, context, d_query,
):
    texts = text_in()[...].reshape(PAIRS * LT, D)
    query.ref[...] = mm(texts, wq_in()[...]).astype(BF)
    query.send()
    every = list(range(PAIRS))
    attend(every, every, keys_t_in(), values_in(), query.ref, weights, probs.ref, context)
    probs.send()
    wo = wo_in()[...]
    wo_t_o.ref[...] = wo.T
    wo_t_o.send()
    summed = mm(context[...], wo) + texts.astype(F32)
    cots = cot_in()[...].reshape(PAIRS * LT, D).astype(F32)
    d_summed = norm_back(summed, cots, gain_in()[...].reshape(1, D))
    d_context.ref[...] = mm(d_summed.astype(BF), wo_t_o.ref[...]).astype(BF)
    d_context.send()
    wq_t_o.ref[...] = wq_in()[...].T
    wq_t_o.send()
    attend_back(
        every, every, keys_in(), values_t_in(), d_context.ref, weights, d_scores.ref, d_query
    )
    d_scores.send()
    grad_o.ref[...] = d_summed + mm(d_query[...], wq_t_o.ref[...])
    grad_o.send()
    total = DEVS * PAIRS
    got = got_in()[...].astype(F32)
    feats_o.ref[...] = got[:, 4:8].reshape(total, TILE).astype(BF)
    feats_o.send()
    _, key_row, local_row = rank_pairs(got[:, :4].reshape(total, TILE))
    mine = (iota((PUSH, total), 0) + PUSH * me_in()[0]).astype(F32) == key_row
    live = jnp.sum(jnp.where(mine, 1.0, 0.0), axis=1, keepdims=True)
    target = jnp.sum(jnp.where(mine, local_row, 0.0), axis=1, keepdims=True)
    meta = jnp.where(live > 0, target, -1.0).astype(jnp.int32)
    meta_o.ref[...] = jnp.broadcast_to(meta, (PUSH, TILE))
    meta_o.send()
    wk_t_o.ref[...] = wk_in()[...].T
    wk_t_o.send()
    wv_t_o.ref[...] = wv_in()[...].T
    wv_t_o.send()


def guest_kernel(
    got_in, meta_in, cot_in, wq_in, keys_t_in, values_in, wo_in, gain_in,
    wo_t_in, values_t_in, keys_in, wq_t_in,
    out, query, probs, d_context, d_scores, feats_o,
    weights, context, d_query, texts, cots, d_summed_ref,
):
    count = PUSH + PAIRS
    tiles = count // PAIRS
    out.ref[PIECES * tiles :] = jnp.zeros(((DEVS - PIECES) * tiles, PAIRS, TILE), BF)
    out.send(PIECES * tiles, DEVS * tiles)
    out_row = iota((20 * LT, 24 * LT), 0)
    in_row = iota((20 * LT, 24 * LT), 1)
    perm = one_hot(in_row == (out_row & 15) * 24 + (out_row >> 4))
    got_ref = got_in()
    parts = []
    for c in range(COLS):
        got = got_ref[c * LT : (c + 1) * LT].astype(F32)
        parts.append(got.reshape(LT * 24, TILE).astype(BF))
    pieces = jnp.concatenate(parts, axis=1)
    rows = mm(perm, pieces)
    push_rows = PUSH * LT
    texts[:push_rows] = rows[:push_rows].astype(BF)
    texts[push_rows:] = rows[2 * push_rows :].astype(BF)
    cots[:push_rows] = rows[push_rows : 2 * push_rows].astype(BF)
    cots[push_rows:] = cot_in()[...].reshape(PAIRS * LT, D)
    feats = got_ref[:, 16:24].astype(F32)[:, PAIRS:]
    feats_o.ref[...] = feats.reshape(DEVS * PAIRS, TILE).astype(BF)
    feats_o.send()
    query.ref[...] = mm(texts[...], wq_in()[...]).astype(BF)
    query.send()
    meta = meta_in()
    own = list(range(PAIRS))
    keys_t, values = keys_t_in(), values_in()

    items = list(range(count))
    targets = [jnp.maximum(meta[i, 0], 0) for i in range(PUSH)] + own
    attend(items, targets, keys_t, values, query.ref, weights, probs.ref, context)
    probs.send()
    summed = mm(context[...], wo_in()[...]) + texts[...].astype(F32)
    d_summed = norm_back(summed, cots[...].astype(F32), gain_in()[...].reshape(1, D))
    d_summed_ref[...] = d_summed
    d_context.ref[...] = mm(d_summed.astype(BF), wo_t_in()[...]).astype(BF)
    d_context.send()
    keys, values_t = keys_in(), values_t_in()

    attend_back(items, targets, keys, values_t, d_context.ref, weights, d_scores.ref, d_query)
    d_scores.send()
    grads = (d_summed_ref[...] + mm(d_query[...], wq_t_in()[...])).astype(BF)
    out_row = iota((LT * count, count * LT), 0)
    in_row = iota((LT * count, count * LT), 1)
    row = out_row // count
    perm = one_hot(in_row == (out_row - row * count) * LT + row)
    back = mm(perm, grads)
    for c in range(COLS):
        block = slice(c * LT * tiles, (c + 1) * LT * tiles)
        part = back[:, c * TILE : (c + 1) * TILE]
        out.ref[block] = part.reshape(LT * tiles, PAIRS, TILE).astype(BF)
        out.send(block.start, block.stop)


def image_kernel(
    own_ds_in, own_q_in, ds_in, q_in, own_p_in, own_dc_in, p_in, dc_in, meta_in, wk_t_in, wv_t_in,
    out, d_keys, d_values, made,
):
    mask = head_mask()
    meta = meta_in()
    targets = [jnp.maximum(meta[i, 0], 0) for i in range(PUSH)]
    sides = (
        (d_keys, own_ds_in, own_q_in, ds_in, q_in),
        (d_values, own_p_in, own_dc_in, p_in, dc_in),
    )
    for total, own_left_in, own_right_in, left_in, right_in in sides:
        own_left, own_right, left, right = own_left_in(), own_right_in(), left_in(), right_in()
        for g in range(GROUPS):
            cols = slice(g * GW, (g + 1) * GW)
            rows = slice(g * GR, (g + 1) * GR)
            for t in range(PAIRS):
                at = slice(t * LT, (t + 1) * LT)
                pat = slice((PUSH + t) * LT, (PUSH + t + 1) * LT)
                total[t, :, cols] = mm(
                    jnp.concatenate([own_left[t, rows, :], left[PUSH + t, rows, :]], axis=0),
                    jnp.concatenate(
                        [spread(own_right[at, cols], mask), spread(right[pat, cols], mask)], axis=0
                    ),
                    TN,
                )
            for i in range(PUSH):
                at = slice(i * LT, (i + 1) * LT)
                total[targets[i], :, cols] += mm(
                    left[i, rows, :], spread(right[at, cols], mask), TN
                )
    d_keys_half = d_keys[...].astype(BF).reshape(PAIRS * LIR, D)
    d_values_half = d_values[...].astype(BF).reshape(PAIRS * LIR, D)
    wk_t, wv_t = wk_t_in(), wv_t_in()
    for g in range(GROUPS):
        cols = slice(g * GW, (g + 1) * GW)
        rows = mm(d_keys_half, wk_t[:, cols]) + mm(d_values_half, wv_t[:, cols])
        for t in range(PAIRS):
            made[:, t, cols] = rows[t * LIR : t * LIR + LI]
    out.ref[...] = made[...].astype(BF)
    out.send()


def log_sums(table):
    peak = jnp.max(table, axis=0, keepdims=True)
    return peak + jnp.log(jnp.sum(jnp.exp(table - peak), axis=0, keepdims=True))


def contrast_kernel(
    mine_a, mine_b, other_a, other_b, tf_in, if_in, me_in, d_text_o, d_image_o
):
    total = DEVS * PAIRS
    me = me_in()[0]
    mine = jnp.concatenate([mine_a()[...], mine_b()[...]], axis=1)
    other = jnp.concatenate([other_a()[...], other_b()[...]], axis=1)
    even = (me & 1) == 0
    texts = jnp.where(even, mine, other)
    images = jnp.where(even, other, mine)
    texts_t, images_t = texts.T, images.T
    row_lse = log_sums(mm(images, texts_t) * SIM_SCALE)
    col_lse = log_sums(mm(texts, images_t) * SIM_SCALE)
    own = iota((PAIRS, total), 0) + me * PAIRS == iota((PAIRS, total), 1)

    def side(rows_in, turned, plain, across_lse, o):
        similar = mm(rows_in()[...], turned) * SIM_SCALE
        peak = jnp.max(similar, axis=1, keepdims=True)
        own_lse = peak + jnp.log(jnp.sum(jnp.exp(similar - peak), axis=1, keepdims=True))
        d_similar = 0.5 * jnp.exp(similar - own_lse) + 0.5 * jnp.exp(similar - across_lse)
        d_similar = d_similar - jnp.where(own, 1.0, 0.0)
        high = d_similar.astype(BF)
        rest = d_similar - high.astype(F32)
        middle = rest.astype(BF)
        low = (rest - middle.astype(F32)).astype(BF)
        o.ref[...] = SIM_SCALE * (mm(high, plain) + (mm(middle, plain) + mm(low, plain)))
        o.send()

    side(tf_in, images_t, images, col_lse, d_text_o)
    side(if_in, texts_t, texts, row_lse, d_image_o)


class Loaded:
    def __init__(self, src, dst, sem):
        self.copy = pltpu.make_async_copy(src, dst, sem)
        self.copy.start()
        self.buffer = dst
        self.waited = False

    def __call__(self):
        if not self.waited:
            self.copy.wait()
            self.waited = True
        return self.buffer


class Direct:
    def __init__(self, ref):
        self.buffer = ref

    def __call__(self):
        return self.buffer


class Stored:
    def __init__(self, ref, dst, sems, first):
        self.ref, self.dst, self.sems, self.first = ref, dst, sems, first
        self.copies = []

    def send(self, begin=None, end=None):
        ref, dst = self.ref, self.dst
        if begin is not None:
            ref, dst = ref.at[begin:end], dst.at[begin:end]
        copy = pltpu.make_async_copy(ref, dst, self.sems.at[self.first + len(self.copies)])
        copy.start()
        self.copies.append(copy)


def call(kernel, outs, args, scratch=(), flops=0, name=None, scalars=(), direct=(), mib=56):
    shapes = [jax.ShapeDtypeStruct(s, d) for s, d in outs]
    n, m = len(args), len(outs)
    size = sum(a.size * a.dtype.itemsize for a in args)
    size += sum(math.prod(s.shape) * s.dtype.itemsize for s in shapes)
    loaded = [k for k in range(n) if k not in direct]

    def body(*refs):
        arrays, refs = refs[: n + m], refs[n + m :]
        buffers, refs = refs[: len(loaded) + m], refs[len(loaded) + m :]
        sems, rest = refs[0], refs[1:]
        operands = [Direct(array) for array in arrays[:n]]
        for slot, k in enumerate(loaded):
            operands[k] = Loaded(arrays[k], buffers[slot], sems.at[slot])
        stores = [
            Stored(buffers[len(loaded) + k], arrays[n + k], sems, n + k * SEND_PARTS)
            for k in range(m)
        ]
        kernel(*operands, *stores, *rest)
        for operand in operands:
            operand()
        for store in stores:
            for copy in store.copies:
                copy.wait()

    buffers = [
        (pltpu.SMEM if k in scalars else pltpu.VMEM)(args[k].shape, args[k].dtype) for k in loaded
    ]
    buffers += [pltpu.VMEM(s.shape, s.dtype) for s in shapes]
    far = pl.BlockSpec(memory_space=pltpu.HBM)
    near = pl.BlockSpec(memory_space=pltpu.VMEM)
    return pl.pallas_call(
        body,
        out_shape=shapes,
        in_specs=[near if k in direct else far for k in range(n)],
        out_specs=[far] * m,
        scratch_shapes=buffers
        + [pltpu.SemaphoreType.DMA((n + m * SEND_PARTS,))]
        + list(scratch),
        compiler_params=pltpu.CompilerParams(vmem_limit_bytes=mib * MIB),
        cost_estimate=pl.CostEstimate(flops=flops, bytes_accessed=size, transcendentals=0),
        name=name,
    )(*args)


def exchange(x):
    return lax.all_to_all(x, "dp", split_axis=0, concat_axis=0, tiled=True)


def on_device(
    text_states, image_states, cot_positive, cot_neg_image, cot_neg_text,
    w_query, w_key, w_value, w_out, ln_gain, neg_image, neg_text, text_feat, image_feat,
):
    me = lax.axis_index("dp").astype(jnp.int32).reshape(1)
    count = PUSH + PAIRS
    (send,) = call(
        pack_kernel,
        [((DEVS, 16, TILE), BF)],
        (neg_image, neg_text, text_feat, image_feat, text_states, cot_neg_image),
        name="pack",
        scalars=(0, 1),
    )
    got = exchange(send)
    image_rows = ((PAIRS, LIR, D), BF)
    image_cols = ((PAIRS, D, LIR), BF)
    keys, values, keys_t, values_t = call(
        project_kernel,
        [image_rows, image_rows, image_cols, image_cols],
        (image_states, w_key, w_value),
        [pltpu.VMEM((PAIRS * LIR, D), BF)],
        flops=4 * PAIRS * LIR * D * D,
        name="project",
    )
    got, keys = lax.optimization_barrier((got, keys))
    feat_half = ((DEVS * PAIRS, TILE), BF)
    send, ids = call(
        pick_kernel,
        [((DEVS, 24, TILE), BF), ((DEVS * PAIRS, TILE), BF)],
        (got, text_feat, image_feat),
        [pltpu.VMEM((DEVS * PAIRS, 2 * TILE), BF)],
        name="pick",
        direct=(0,),
        mib=16,
    )
    send, keys = lax.optimization_barrier((send, keys))
    got_rows = exchange(send)
    square = ((D, D), BF)
    own_grad, own_ds, own_p, own_q, own_dc, wo_t, wq_t, wk_t, wv_t, meta, feats_a = call(
        own_kernel,
        [
            ((PAIRS * LT, D), F32),
            ((PAIRS, H * LT, LIR), BF),
            ((PAIRS, H * LT, LIR), BF),
            ((PAIRS * LT, D), BF),
            ((PAIRS * LT, D), BF),
            square,
            square,
            square,
            square,
            ((PUSH, TILE), jnp.int32),
            feat_half,
        ],
        (
            text_states, w_query, keys_t, values, w_out, ln_gain, cot_positive,
            values_t, keys, me, got, w_key, w_value,
        ),
        [
            pltpu.VMEM((PAIRS, H * LT, LIR), F32),
            pltpu.VMEM((PAIRS * LT, D), BF),
            pltpu.VMEM((PAIRS * LT, D), BF),
        ],
        flops=8 * PAIRS * LT * D * D * 4,
        name="own",
        scalars=(9,),
        mib=63,
    )
    swap = [(i, i ^ 1) for i in range(DEVS)]
    swapped_a = lax.ppermute(feats_a, "dp", swap)
    got_rows, own_grad = lax.optimization_barrier((got_rows, own_grad))
    send, q, p, dc, ds, feats_b = call(
        guest_kernel,
        [
            ((DEVS * count // PAIRS, PAIRS, TILE), BF),
            ((count * LT, D), BF),
            ((count, H * LT, LIR), BF),
            ((count * LT, D), BF),
            ((count, H * LT, LIR), BF),
            feat_half,
        ],
        (
            got_rows, meta, cot_neg_text, w_query, keys_t, values, w_out, ln_gain,
            wo_t, values_t, keys, wq_t,
        ),
        [
            pltpu.VMEM((count, H * LT, LIR), F32),
            pltpu.VMEM((count * LT, D), BF),
            pltpu.VMEM((count * LT, D), BF),
            pltpu.VMEM((count * LT, D), BF),
            pltpu.VMEM((count * LT, D), BF),
            pltpu.VMEM((count * LT, D), F32),
        ],
        flops=8 * count * LT * D * D * 4,
        name="guest",
        scalars=(1,),
    )
    got_back = exchange(send)
    swapped_b = lax.ppermute(feats_b, "dp", swap)
    (d_image,) = call(
        image_kernel,
        [((LI, PAIRS, D), BF)],
        (own_ds, own_q, ds, q, own_p, own_dc, p, dc, meta, wk_t, wv_t),
        [
            pltpu.VMEM((PAIRS, LIR, D), F32),
            pltpu.VMEM((PAIRS, LIR, D), F32),
            pltpu.VMEM((LI, PAIRS, D), F32),
        ],
        flops=8 * PAIRS * LIR * D * D,
        name="image",
        scalars=(8,),
    )
    got_back, d_image, swapped_b = lax.optimization_barrier((got_back, d_image, swapped_b))
    (send,) = call(sum_kernel, [((DEVS, PAIRS, TILE), BF)], (ids, got_back), name="sum", direct=(1,), mib=16)
    send, swapped_b = lax.optimization_barrier((send, swapped_b))
    got_sum = exchange(send)
    d_text_feat, d_image_feat = call(
        contrast_kernel,
        [((PAIRS, E), F32), ((PAIRS, E), F32)],
        (feats_a, feats_b, swapped_a, swapped_b, text_feat, image_feat, me),
        flops=8 * 512 * 512 * 256,
        name="contrast",
        scalars=(6,),
    )
    got_sum, d_text_feat, d_image_feat = lax.optimization_barrier(
        (got_sum, d_text_feat, d_image_feat)
    )
    (d_text,) = call(join_kernel, [((PAIRS, LT, D), BF)], (own_grad, got_sum), name="join", direct=(1,), mib=16)
    return (d_text, jnp.transpose(d_image, (1, 0, 2)), d_text_feat, d_image_feat)


def solution(mesh):
    return jax.shard_map(
        on_device,
        mesh=mesh,
        in_specs=(
            P("dp", None, None),
            P("dp", None, None),
            P("dp", None, None),
            P("dp", None, None),
            P("dp", None, None),
            P(),
            P(),
            P(),
            P(),
            P(),
            P("dp"),
            P("dp"),
            P("dp", None),
            P("dp", None),
        ),
        out_specs=(P("dp", None, None), P("dp", None, None), P("dp", None), P("dp", None)),
        check_vma=False,
    )
```

```python
import math

import jax
import jax.numpy as jnp
from jax import lax
from jax.experimental import pallas as pl
from jax.experimental.pallas import tpu as pltpu
from jax.sharding import PartitionSpec as P

D = 768
H = 12
E = 256
LT = 16
LI = 197
PAIRS = 4
DEVS = 128
TILE = 128
COLS = D // TILE
PIECES = COLS * LT
LIR = 208
GROUP = 4
GROUPS = H // GROUP
GW = D // GROUPS
GR = GROUP * LT
INV_ROOT = 1.0 / math.sqrt(D // H)
NORM_EPS = 1e-06
SIM_SCALE = 3.0 / math.sqrt(E)
PUSH = 2 * PAIRS
SLOT1 = 4
BF = jnp.bfloat16
F32 = jnp.float32
MIB = 1024 * 1024
SEND_PARTS = 8

NN = (((1,), (0,)), ((), ()))
NT = (((1,), (1,)), ((), ()))
TN = (((0,), (0,)), ((), ()))


def mm(a, b, dims=NN):
    return lax.dot_general(a, b, dims, preferred_element_type=F32)


def iota(shape, dim):
    return lax.broadcasted_iota(jnp.int32, shape, dim)


def one_hot(mask):
    return jnp.where(mask, 1.0, 0.0).astype(BF)


def pack_kernel(ni_in, nt_in, tf_in, if_in, text_in, cot_in, out):
    out_row = iota((TILE, TILE), 0)
    in_row = iota((TILE, TILE), 1)
    perm = one_hot(in_row == (out_row & 7) * LT + (out_row >> 3))
    row = iota((PAIRS, TILE), 0)
    lane = iota((PAIRS, TILE), 1)
    ni_ref, nt_ref = ni_in(), nt_in()
    ids = jnp.zeros((PAIRS, TILE), jnp.int32)
    for a in range(PAIRS):
        ni = ni_ref[a]
        nt = nt_ref[a]
        for j, val in enumerate((ni >> 2, ni & 3, nt >> 2, nt & 3)):
            ids = jnp.where(jnp.logical_and(row == a, lane == j), val, ids)
    ids = ids.astype(F32)
    tf = tf_in()[...].astype(F32)
    im = if_in()[...].astype(F32)
    place = iota((LT, PAIRS, TILE), 0) & 3
    feats = jnp.where(place == 1, im[:, :TILE][None], tf[:, :TILE][None])
    feats = jnp.where(place == 2, tf[:, TILE:][None], feats)
    feats = jnp.where(place == 3, im[:, TILE:][None], feats)
    shared = [jnp.broadcast_to(ids[None], (LT, PAIRS, TILE)), feats]
    rows = jnp.concatenate([text_in()[...], cot_in()[...]], axis=0).reshape(TILE, D)
    pieces = mm(perm, rows)

    def put(c, part):
        tiles = [t[:, None] for t in shared] + [part.reshape(LT, 2, PAIRS, TILE)]
        slots = jnp.concatenate(tiles, axis=1).astype(BF)
        out.ref[c * LT * SLOT1 : (c + 1) * LT * SLOT1] = slots.reshape(LT * SLOT1, PAIRS, TILE)

    for c in range(COLS):
        put(c, pieces[:, c * TILE : (c + 1) * TILE])
        out.send(c * LT * SLOT1, (c + 1) * LT * SLOT1)
    for c in range(COLS, DEVS // LT):
        put(c, jnp.zeros((TILE, TILE), F32))
    out.send(PIECES * SLOT1, DEVS * SLOT1)


def column_to_row(rows, *lanes):
    pick = jnp.zeros((8, TILE), BF)
    for k, lane in enumerate(lanes):
        here = jnp.logical_and(iota((8, TILE), 0) == k, iota((8, TILE), 1) == lane)
        pick = pick + one_hot(here)
    return mm(pick, rows, NT)


def rank_pairs(ids):
    total = DEVS * PAIRS
    owner_col = ids[:, 0:1]
    owner_row = column_to_row(ids.astype(BF), 0)[0:1]
    step = 128
    ranks = []
    for b in range(total // step):
        earlier = iota((step, total), 1) < iota((step, total), 0) + b * step
        same = owner_col[b * step : (b + 1) * step] == owner_row
        ranks.append(
            jnp.sum(jnp.where(jnp.logical_and(same, earlier), 1.0, 0.0), axis=1, keepdims=True)
        )
    rank_col = jnp.concatenate(ranks, axis=0)
    with_rank = jnp.where(iota((total, TILE), 1) == 4, rank_col, ids).astype(BF)
    flat = column_to_row(with_rank, 0, 1, 4)
    return with_rank, flat[0:1] * PUSH + flat[2:3], flat[1:2]


def tile_rows(ref, k):
    tiles = ref[...].reshape(DEVS, SLOT1, PAIRS, TILE)[:, k]
    return tiles.astype(F32).reshape(DEVS * PAIRS, TILE)


def pick_kernel(got_in, out, ids_out, pair_tab):
    total = DEVS * PAIRS
    got = got_in()
    ids = tile_rows(got, 0)
    pair_tab[:, :TILE] = tile_rows(got, 2).astype(BF)
    pair_tab[:, TILE:] = tile_rows(got, 3).astype(BF)
    target_col = ids[:, 2:3] * PAIRS + ids[:, 3:4]
    with_rank, key_row, _ = rank_pairs(ids)
    ids_out.ref[...] = with_rank
    ids_out.send()
    slot_col = iota((DEVS * PUSH, 1), 0).astype(F32)
    pair_row = iota((1, total), 1).astype(F32)
    devs = 32
    for b in range(DEVS // devs):
        slots = slice(b * devs * PUSH, (b + 1) * devs * PUSH)
        pairs = slice(b * devs * PAIRS, (b + 1) * devs * PAIRS)
        pushed = mm(one_hot(slot_col[slots] == key_row), pair_tab[...])
        pulled = mm(one_hot(target_col[pairs] == pair_row), pair_tab[:, :TILE])
        tiles = jnp.concatenate(
            [
                pushed[:, :TILE].reshape(devs, 2, PAIRS, TILE),
                pushed[:, TILE:].reshape(devs, 2, PAIRS, TILE),
                pulled.reshape(devs, 1, PAIRS, TILE),
            ],
            axis=1,
        ).astype(BF)
        out.ref[b * devs * 5 : (b + 1) * devs * 5] = tiles.reshape(devs * 5, PAIRS, TILE)
        out.send(b * devs * 5, (b + 1) * devs * 5)


def sum_kernel(ids_in, got_in, out):
    total = DEVS * PAIRS
    ids_ref = ids_in()
    ids = ids_ref[...].astype(F32)
    key_col = ids[:, 0:1] * PUSH + ids[:, 4:5]
    flat = column_to_row(ids_ref[...], 2, 3)
    target_row = flat[0:1] * PAIRS + flat[1:2]
    pair_col = iota((total, 1), 0).astype(F32)
    slot_row = iota((1, DEVS * PUSH), 1).astype(F32)
    got = got_in()[...].astype(F32).reshape(DEVS, PUSH + PAIRS, TILE)
    push = got[:, :PUSH].reshape(DEVS * PUSH, TILE).astype(BF)
    pull = got[:, PUSH:].reshape(total, TILE).astype(BF)
    devs = 32
    for b in range(DEVS // devs):
        block = slice(b * devs * PAIRS, (b + 1) * devs * PAIRS)
        both = mm(one_hot(key_col[block] == slot_row), push)
        both += mm(one_hot(pair_col[block] == target_row), pull)
        out.ref[b * devs : (b + 1) * devs] = both.reshape(devs, PAIRS, TILE).astype(BF)
        out.send(b * devs, (b + 1) * devs)


def join_kernel(own_in, got_in, out):
    parts = []
    got_ref = got_in()
    for c in range(COLS):
        got = got_ref[c * LT : (c + 1) * LT].astype(F32)
        parts.append(got.reshape(LT * PAIRS, TILE).astype(BF))
    pieces = jnp.concatenate(parts, axis=1)
    out_row = iota((PAIRS * LT, LT * PAIRS), 0)
    in_row = iota((PAIRS * LT, LT * PAIRS), 1)
    perm = one_hot(in_row == (out_row & 15) * PAIRS + (out_row >> 4))
    total = own_in()[...] + mm(perm, pieces)
    out.ref[...] = total.astype(BF).reshape(PAIRS, LT, D)
    out.send()


def head_mask(scale=1.0):
    same = (iota((GR, GW), 0) >> 4) == (iota((GR, GW), 1) >> 6)
    return jnp.where(same, scale, 0.0).astype(BF)


def spread(rows, mask):
    return jnp.concatenate([rows] * GROUP, axis=0) * mask


def fold(full):
    head = iota((LT, GW), 1) >> 6
    out = full[0:LT]
    for h in range(1, GROUP):
        out = jnp.where(head == h, full[h * LT : (h + 1) * LT], out)
    return out


def parts_of(items, targets):
    for i, target in zip(items, targets):
        at = slice(i * LT, (i + 1) * LT)
        for g in range(GROUPS):
            yield i, target, at, slice(g * GW, (g + 1) * GW), slice(g * GR, (g + 1) * GR)


def attend(items, targets, keys_t, values, query, weights, probs, context):
    mask = head_mask(INV_ROOT)
    lane = iota((GR, LIR), 1)
    work = list(parts_of(items, targets))
    scores = []
    for i, target, at, cols, rows in work:
        s = mm(spread(query[at, cols], mask), keys_t[target, cols, :])
        scores.append(jnp.where(lane < LI, s, -1e30))
    halves = []
    for (i, target, at, cols, rows), s in zip(work, scores):
        w = jnp.exp(s - jnp.max(s, axis=1, keepdims=True))
        w = w * (1.0 / jnp.sum(w, axis=1, keepdims=True))
        half = w.astype(BF)
        weights[i, rows, :] = w
        probs[i, rows, :] = half
        halves.append(half)
    for (i, target, at, cols, rows), half in zip(work, halves):
        context[at, cols] = fold(mm(half, values[target, :, cols])).astype(BF)


def attend_back(items, targets, keys, values_t, d_context, weights, d_scores, d_query):
    mask = head_mask(INV_ROOT)
    work = list(parts_of(items, targets))
    d_probs = []
    for i, target, at, cols, rows in work:
        d_probs.append(mm(spread(d_context[at, cols], mask), values_t[target, cols, :]))
    halves = []
    for (i, target, at, cols, rows), dp in zip(work, d_probs):
        w = weights[i, rows, :]
        ds = w * (dp - jnp.sum(w * dp, axis=1, keepdims=True))
        ds = ds.astype(BF)
        d_scores[i, rows, :] = ds
        halves.append(ds)
    for (i, target, at, cols, rows), ds in zip(work, halves):
        d_query[at, cols] = fold(mm(ds, keys[target, :, cols])).astype(BF)


def norm_back(summed, cot, gain):
    centred = summed - jnp.mean(summed, axis=1, keepdims=True)
    inv_sigma = lax.rsqrt(jnp.mean(centred * centred, axis=1, keepdims=True) + NORM_EPS)
    normed = centred * inv_sigma
    gz = cot * gain
    return inv_sigma * (
        gz
        - jnp.mean(gz, axis=1, keepdims=True)
        - normed * jnp.mean(gz * normed, axis=1, keepdims=True)
    )


def project_kernel(
    image_in, wk_in, wv_in, keys_o, values_o, keys_t_o, values_t_o, wk_t_o, wv_t_o, padded
):
    image = image_in()
    padded[...] = jnp.zeros_like(padded)
    for t in range(PAIRS):
        padded[t * LIR : t * LIR + LI] = image[t]
    for w_in, plain, turned, w_t in (
        (wk_in, keys_o, keys_t_o, wk_t_o),
        (wv_in, values_o, values_t_o, wv_t_o),
    ):
        w = w_in()
        w_t.ref[...] = w[...].T
        w_t.send()
        for g in range(GROUPS):
            cols = slice(g * GW, (g + 1) * GW)
            made = mm(padded[...], w[:, cols]).astype(BF)
            for t in range(PAIRS):
                rows = made[t * LIR : (t + 1) * LIR]
                plain.ref[t, :, cols] = rows
                turned.ref[t, cols, :] = rows.T
        plain.send()
        turned.send()


def own_kernel(
    text_in, wq_in, keys_t_in, values_in, wo_in, gain_in, cot_in, values_t_in, keys_in,
    me_in, got_in,
    grad_o, d_scores, probs, query, d_context, meta_o, feats_o,
    weights, context, d_query,
):
    texts = text_in()[...].reshape(PAIRS * LT, D)
    query.ref[...] = mm(texts, wq_in()[...]).astype(BF)
    query.send()
    every = list(range(PAIRS))
    attend(every, every, keys_t_in(), values_in(), query.ref, weights, probs.ref, context)
    probs.send()
    wo = wo_in()[...]
    summed = mm(context[...], wo) + texts.astype(F32)
    cots = cot_in()[...].reshape(PAIRS * LT, D).astype(F32)
    d_summed = norm_back(summed, cots, gain_in()[...].reshape(1, D))
    d_context.ref[...] = mm(d_summed.astype(BF), wo.T).astype(BF)
    d_context.send()
    attend_back(
        every, every, keys_in(), values_t_in(), d_context.ref, weights, d_scores.ref, d_query
    )
    d_scores.send()
    grad_o.ref[...] = d_summed + mm(d_query[...], wq_in()[...].T)
    grad_o.send()
    total = DEVS * PAIRS
    got = got_in()
    feats_o.ref[...] = tile_rows(got, 1).astype(BF)
    feats_o.send()
    _, key_row, local_row = rank_pairs(tile_rows(got, 0))
    mine = (iota((PUSH, total), 0) + PUSH * me_in()[0]).astype(F32) == key_row
    live = jnp.sum(jnp.where(mine, 1.0, 0.0), axis=1, keepdims=True)
    target = jnp.sum(jnp.where(mine, local_row, 0.0), axis=1, keepdims=True)
    meta = jnp.where(live > 0, target, -1.0).astype(jnp.int32)
    meta_o.ref[...] = jnp.broadcast_to(meta, (PUSH, TILE))
    meta_o.send()


def guest_kernel(
    got_in, meta_in, cot_in, wq_in, keys_t_in, values_in, wo_in, gain_in,
    values_t_in, keys_in,
    out, query, probs, d_context, d_scores,
    weights, context, d_query, texts, cots, d_summed_ref,
):
    count = PUSH + PAIRS
    tiles = count // PAIRS
    out.ref[PIECES * tiles :] = jnp.zeros(((DEVS - PIECES) * tiles, PAIRS, TILE), BF)
    out.send(PIECES * tiles, DEVS * tiles)
    out_row = iota((20 * LT, 20 * LT), 0)
    in_row = iota((20 * LT, 20 * LT), 1)
    perm = one_hot(in_row == (out_row & 15) * 20 + (out_row >> 4))
    got_ref = got_in()
    parts = []
    for c in range(COLS):
        got = got_ref[c * LT * 5 : (c + 1) * LT * 5].astype(F32)
        parts.append(got.reshape(LT * 20, TILE).astype(BF))
    pieces = jnp.concatenate(parts, axis=1)
    rows = mm(perm, pieces)
    push_rows = PUSH * LT
    texts[:push_rows] = rows[:push_rows].astype(BF)
    texts[push_rows:] = rows[2 * push_rows :].astype(BF)
    cots[:push_rows] = rows[push_rows : 2 * push_rows].astype(BF)
    cots[push_rows:] = cot_in()[...].reshape(PAIRS * LT, D)
    wq = wq_in()[...]
    query.ref[...] = mm(texts[...], wq).astype(BF)
    query.send()
    meta = meta_in()
    own = list(range(PAIRS))
    keys_t, values = keys_t_in(), values_in()

    items = list(range(count))
    targets = [jnp.maximum(meta[i, 0], 0) for i in range(PUSH)] + own
    attend(items, targets, keys_t, values, query.ref, weights, probs.ref, context)
    probs.send()
    wo = wo_in()[...]
    summed = mm(context[...], wo) + texts[...].astype(F32)
    d_summed = norm_back(summed, cots[...].astype(F32), gain_in()[...].reshape(1, D))
    d_summed_ref[...] = d_summed
    d_context.ref[...] = mm(d_summed.astype(BF), wo.T).astype(BF)
    d_context.send()
    keys, values_t = keys_in(), values_t_in()

    attend_back(items, targets, keys, values_t, d_context.ref, weights, d_scores.ref, d_query)
    d_scores.send()
    grads = (d_summed_ref[...] + mm(d_query[...], wq.T)).astype(BF)
    out_row = iota((LT * count, count * LT), 0)
    in_row = iota((LT * count, count * LT), 1)
    row = out_row // count
    perm = one_hot(in_row == (out_row - row * count) * LT + row)
    back = mm(perm, grads)
    for c in range(COLS):
        block = slice(c * LT * tiles, (c + 1) * LT * tiles)
        part = back[:, c * TILE : (c + 1) * TILE]
        out.ref[block] = part.reshape(LT * tiles, PAIRS, TILE).astype(BF)
        out.send(block.start, block.stop)


def image_kernel(
    own_ds_in, own_q_in, ds_in, q_in, own_p_in, own_dc_in, p_in, dc_in, meta_in, wk_t_in, wv_t_in,
    out, d_keys, d_values,
):
    mask = head_mask()
    meta = meta_in()
    targets = [jnp.maximum(meta[i, 0], 0) for i in range(PUSH)]
    sides = (
        (d_keys, own_ds_in, own_q_in, ds_in, q_in),
        (d_values, own_p_in, own_dc_in, p_in, dc_in),
    )
    for total, own_left_in, own_right_in, left_in, right_in in sides:
        own_left, own_right, left, right = own_left_in(), own_right_in(), left_in(), right_in()
        for g in range(GROUPS):
            cols = slice(g * GW, (g + 1) * GW)
            rows = slice(g * GR, (g + 1) * GR)
            for t in range(PAIRS):
                at = slice(t * LT, (t + 1) * LT)
                pat = slice((PUSH + t) * LT, (PUSH + t + 1) * LT)
                total[t, :, cols] = mm(
                    jnp.concatenate([own_left[t, rows, :], left[PUSH + t, rows, :]], axis=0),
                    jnp.concatenate(
                        [spread(own_right[at, cols], mask), spread(right[pat, cols], mask)], axis=0
                    ),
                    TN,
                )
            for i in range(PUSH):
                at = slice(i * LT, (i + 1) * LT)
                total[targets[i], :, cols] += mm(
                    left[i, rows, :], spread(right[at, cols], mask), TN
                )
    d_keys_half = d_keys[...].astype(BF).reshape(PAIRS * LIR, D)
    d_values_half = d_values[...].astype(BF).reshape(PAIRS * LIR, D)
    wk_t, wv_t = wk_t_in(), wv_t_in()
    for g in range(GROUPS):
        cols = slice(g * GW, (g + 1) * GW)
        rows = mm(d_keys_half, wk_t[:, cols]) + mm(d_values_half, wv_t[:, cols])
        for t in range(PAIRS):
            out.ref[t, :, cols] = rows[t * LIR : (t + 1) * LIR].astype(BF)[:LI]
    out.send()


def log_sums(table):
    peak = jnp.max(table, axis=0, keepdims=True)
    return peak + jnp.log(jnp.sum(jnp.exp(table - peak), axis=0, keepdims=True))


def contrast_kernel(mine_in, by1_in, by2_in, by3_in, tf_in, if_in, me_in, d_text_o, d_image_o):
    total = DEVS * PAIRS
    me = me_in()[0]
    parts = [o()[...] for o in (mine_in, by1_in, by2_in, by3_in)]
    odd, upper = (me & 1) == 1, (me & 2) == 2
    pairs = [jnp.where(odd, parts[k ^ 1], parts[k]) for k in range(4)]
    texts = jnp.concatenate(
        [jnp.where(upper, pairs[2], pairs[0]), jnp.where(upper, pairs[0], pairs[2])], axis=1
    )
    images = jnp.concatenate(
        [jnp.where(upper, pairs[3], pairs[1]), jnp.where(upper, pairs[1], pairs[3])], axis=1
    )
    texts_t, images_t = texts.T, images.T
    row_lse = log_sums(mm(images, texts_t) * SIM_SCALE)
    col_lse = log_sums(mm(texts, images_t) * SIM_SCALE)
    own = iota((PAIRS, total), 0) + me * PAIRS == iota((PAIRS, total), 1)

    def side(rows_in, turned, plain, across_lse, o):
        similar = mm(rows_in()[...], turned) * SIM_SCALE
        peak = jnp.max(similar, axis=1, keepdims=True)
        own_lse = peak + jnp.log(jnp.sum(jnp.exp(similar - peak), axis=1, keepdims=True))
        d_similar = 0.5 * jnp.exp(similar - own_lse) + 0.5 * jnp.exp(similar - across_lse)
        d_similar = d_similar - jnp.where(own, 1.0, 0.0)
        high = d_similar.astype(BF)
        rest = d_similar - high.astype(F32)
        middle = rest.astype(BF)
        low = (rest - middle.astype(F32)).astype(BF)
        o.ref[...] = SIM_SCALE * (mm(high, plain) + (mm(middle, plain) + mm(low, plain)))
        o.send()

    side(tf_in, images_t, images, col_lse, d_text_o)
    side(if_in, texts_t, texts, row_lse, d_image_o)


class Loaded:
    def __init__(self, src, dst, sem):
        self.copy = pltpu.make_async_copy(src, dst, sem)
        self.buffer = dst
        self.started = self.waited = False

    def start(self):
        if not self.started:
            self.copy.start()
            self.started = True

    def __call__(self):
        self.start()
        if not self.waited:
            self.copy.wait()
            self.waited = True
        return self.buffer


class Direct:
    def __init__(self, ref):
        self.buffer = ref

    def __call__(self):
        return self.buffer


class Stored:
    def __init__(self, ref, dst, sems, first):
        self.ref, self.dst, self.sems, self.first = ref, dst, sems, first
        self.copies = []

    def send(self, begin=None, end=None):
        ref, dst = self.ref, self.dst
        if begin is not None:
            ref, dst = ref.at[begin:end], dst.at[begin:end]
        copy = pltpu.make_async_copy(ref, dst, self.sems.at[self.first + len(self.copies)])
        copy.start()
        self.copies.append(copy)


def call(kernel, outs, args, scratch=(), flops=0, name=None, scalars=(), direct=(), mib=56, late=()):
    shapes = [jax.ShapeDtypeStruct(s, d) for s, d in outs]
    n, m = len(args), len(outs)
    size = sum(a.size * a.dtype.itemsize for a in args)
    size += sum(math.prod(s.shape) * s.dtype.itemsize for s in shapes)
    loaded = [k for k in range(n) if k not in direct]

    def body(*refs):
        arrays, refs = refs[: n + m], refs[n + m :]
        buffers, refs = refs[: len(loaded) + m], refs[len(loaded) + m :]
        sems, rest = refs[0], refs[1:]
        operands = [Direct(array) for array in arrays[:n]]
        for slot, k in enumerate(loaded):
            operands[k] = Loaded(arrays[k], buffers[slot], sems.at[slot])
            if k not in late:
                operands[k].start()
        stores = [
            Stored(buffers[len(loaded) + k], arrays[n + k], sems, n + k * SEND_PARTS)
            for k in range(m)
        ]
        kernel(*operands, *stores, *rest)
        for operand in operands:
            operand()
        for store in stores:
            for copy in store.copies:
                copy.wait()

    buffers = [
        (pltpu.SMEM if k in scalars else pltpu.VMEM)(args[k].shape, args[k].dtype) for k in loaded
    ]
    buffers += [pltpu.VMEM(s.shape, s.dtype) for s in shapes]
    far = pl.BlockSpec(memory_space=pltpu.HBM)
    near = pl.BlockSpec(memory_space=pltpu.VMEM)
    return pl.pallas_call(
        body,
        out_shape=shapes,
        in_specs=[near if k in direct else far for k in range(n)],
        out_specs=[far] * m,
        scratch_shapes=buffers
        + [pltpu.SemaphoreType.DMA((n + m * SEND_PARTS,))]
        + list(scratch),
        compiler_params=pltpu.CompilerParams(vmem_limit_bytes=mib * MIB),
        cost_estimate=pl.CostEstimate(flops=flops, bytes_accessed=size, transcendentals=0),
        name=name,
    )(*args)


def exchange(x):
    return lax.all_to_all(x, "dp", split_axis=0, concat_axis=0, tiled=True)


def on_device(
    text_states, image_states, cot_positive, cot_neg_image, cot_neg_text,
    w_query, w_key, w_value, w_out, ln_gain, neg_image, neg_text, text_feat, image_feat,
):
    me = lax.axis_index("dp").astype(jnp.int32).reshape(1)
    count = PUSH + PAIRS
    (send,) = call(
        pack_kernel,
        [((DEVS * SLOT1, PAIRS, TILE), BF)],
        (neg_image, neg_text, text_feat, image_feat, text_states, cot_neg_image),
        name="pack",
        scalars=(0, 1),
    )
    got = exchange(send)
    image_rows = ((PAIRS, LIR, D), BF)
    image_cols = ((PAIRS, D, LIR), BF)
    square = ((D, D), BF)
    keys, values, keys_t, values_t, wk_t, wv_t = call(
        project_kernel,
        [image_rows, image_rows, image_cols, image_cols, square, square],
        (image_states, w_key, w_value),
        [pltpu.VMEM((PAIRS * LIR, D), BF)],
        flops=4 * PAIRS * LIR * D * D,
        name="project",
    )
    got, keys = lax.optimization_barrier((got, keys))
    send, ids = call(
        pick_kernel,
        [((DEVS * 5, PAIRS, TILE), BF), ((DEVS * PAIRS, TILE), BF)],
        (got,),
        [pltpu.VMEM((DEVS * PAIRS, 2 * TILE), BF)],
        name="pick",
        direct=(0,),
        mib=16,
    )
    send, keys = lax.optimization_barrier((send, keys))
    got_rows = exchange(send)
    own_grad, own_ds, own_p, own_q, own_dc, meta, feats = call(
        own_kernel,
        [
            ((PAIRS * LT, D), F32),
            ((PAIRS, H * LT, LIR), BF),
            ((PAIRS, H * LT, LIR), BF),
            ((PAIRS * LT, D), BF),
            ((PAIRS * LT, D), BF),
            ((PUSH, TILE), jnp.int32),
            ((DEVS * PAIRS, TILE), BF),
        ],
        (
            text_states, w_query, keys_t, values, w_out, ln_gain, cot_positive,
            values_t, keys, me, got,
        ),
        [
            pltpu.VMEM((PAIRS, H * LT, LIR), F32),
            pltpu.VMEM((PAIRS * LT, D), BF),
            pltpu.VMEM((PAIRS * LT, D), BF),
        ],
        flops=8 * PAIRS * LT * D * D * 4,
        name="own",
        scalars=(9,),
        mib=63,
    )
    swapped = [
        lax.ppermute(feats, "dp", [(i, i ^ far) for i in range(DEVS)]) for far in (1, 2, 3)
    ]
    got_rows, own_grad = lax.optimization_barrier((got_rows, own_grad))
    send, q, p, dc, ds = call(
        guest_kernel,
        [
            ((DEVS * count // PAIRS, PAIRS, TILE), BF),
            ((count * LT, D), BF),
            ((count, H * LT, LIR), BF),
            ((count * LT, D), BF),
            ((count, H * LT, LIR), BF),
        ],
        (
            got_rows, meta, cot_neg_text, w_query, keys_t, values, w_out, ln_gain,
            values_t, keys,
        ),
        [
            pltpu.VMEM((count, H * LT, LIR), F32),
            pltpu.VMEM((count * LT, D), BF),
            pltpu.VMEM((count * LT, D), BF),
            pltpu.VMEM((count * LT, D), BF),
            pltpu.VMEM((count * LT, D), BF),
            pltpu.VMEM((count * LT, D), F32),
        ],
        flops=8 * count * LT * D * D * 4,
        name="guest",
        scalars=(1,),
    )
    got_back = exchange(send)
    (d_image,) = call(
        image_kernel,
        [((PAIRS, LI, D), BF)],
        (own_ds, own_q, ds, q, own_p, own_dc, p, dc, meta, wk_t, wv_t),
        [
            pltpu.VMEM((PAIRS, LIR, D), F32),
            pltpu.VMEM((PAIRS, LIR, D), F32),
        ],
        flops=8 * PAIRS * LIR * D * D,
        name="image",
        scalars=(8,),
    )
    got_back, d_image = lax.optimization_barrier((got_back, d_image))
    (send,) = call(sum_kernel, [((DEVS, PAIRS, TILE), BF)], (ids, got_back), name="sum", direct=(1,), mib=16)
    send, *swapped = lax.optimization_barrier((send, *swapped))
    got_sum = exchange(send)
    d_text_feat, d_image_feat = call(
        contrast_kernel,
        [((PAIRS, E), F32), ((PAIRS, E), F32)],
        (feats, *swapped, text_feat, image_feat, me),
        flops=8 * 512 * 512 * 256,
        name="contrast",
        scalars=(6,),
    )
    got_sum, d_text_feat, d_image_feat = lax.optimization_barrier(
        (got_sum, d_text_feat, d_image_feat)
    )
    (d_text,) = call(join_kernel, [((PAIRS, LT, D), BF)], (own_grad, got_sum), name="join", direct=(1,), mib=16)
    return (d_text, d_image, d_text_feat, d_image_feat)


def solution(mesh):
    return jax.shard_map(
        on_device,
        mesh=mesh,
        in_specs=(
            P("dp", None, None),
            P("dp", None, None),
            P("dp", None, None),
            P("dp", None, None),
            P("dp", None, None),
            P(),
            P(),
            P(),
            P(),
            P(),
            P("dp"),
            P("dp"),
            P("dp", None),
            P("dp", None),
        ),
        out_specs=(P("dp", None, None), P("dp", None, None), P("dp", None), P("dp", None)),
        check_vma=False,
    )
```

```python
import math

import jax
import jax.numpy as jnp
from jax import lax
from jax.experimental import pallas as pl
from jax.experimental.pallas import tpu as pltpu
from jax.sharding import PartitionSpec as P

D = 768
H = 12
E = 256
LT = 16
LI = 197
PAIRS = 4
DEVS = 128
TILE = 128
COLS = D // TILE
PIECES = COLS * LT
LIR = 208
GROUP = 4
GROUPS = H // GROUP
GW = D // GROUPS
GR = GROUP * LT
INV_ROOT = 1.0 / math.sqrt(D // H)
NORM_EPS = 1e-06
SIM_SCALE = 3.0 / math.sqrt(E)
PUSH = 2 * PAIRS
SLOT1 = 3
BF = jnp.bfloat16
F32 = jnp.float32
MIB = 1024 * 1024
SEND_PARTS = 8

NN = (((1,), (0,)), ((), ()))
NT = (((1,), (1,)), ((), ()))
TN = (((0,), (0,)), ((), ()))


def mm(a, b, dims=NN):
    return lax.dot_general(a, b, dims, preferred_element_type=F32)


def iota(shape, dim):
    return lax.broadcasted_iota(jnp.int32, shape, dim)


def one_hot(mask):
    return jnp.where(mask, 1.0, 0.0).astype(BF)


def pack_kernel(ni_in, nt_in, tf_in, if_in, text_in, cot_in, out):
    out_row = iota((TILE, TILE), 0)
    in_row = iota((TILE, TILE), 1)
    perm = one_hot(in_row == (out_row & 7) * LT + (out_row >> 3))
    row = iota((PAIRS, TILE), 0)
    lane = iota((PAIRS, TILE), 1)
    ni_ref, nt_ref = ni_in(), nt_in()
    ids = jnp.zeros((PAIRS, TILE), jnp.int32)
    for a in range(PAIRS):
        ni = ni_ref[a]
        nt = nt_ref[a]
        for j, val in enumerate((ni >> 2, ni & 3, nt >> 2, nt & 3)):
            ids = jnp.where(jnp.logical_and(row == a, lane == j), val, ids)
    ids = ids.astype(F32)
    tf = tf_in()[...].astype(F32)
    im = if_in()[...].astype(F32)
    place = iota((LT, PAIRS, TILE), 0) & 7
    feats = jnp.zeros((LT, PAIRS, TILE), F32)
    for q in range(8):
        quarter = q >> 1
        half = (im if q & 1 else tf)[:, (quarter >> 1) * TILE : ((quarter >> 1) + 1) * TILE]
        if quarter & 1 == 0:
            half = jnp.concatenate([half[:, TILE // 2 :], half[:, : TILE // 2]], axis=1)
        feats = jnp.where(place == q, half[None], feats)
    upper = iota((LT, PAIRS, TILE), 2) >= TILE // 2
    shared = [jnp.where(upper, feats, ids[None])]

    def put(c, part):
        tiles = [t[:, None] for t in shared] + [part.reshape(LT, 2, PAIRS, TILE)]
        slots = jnp.concatenate(tiles, axis=1).astype(BF)
        out.ref[c * LT * SLOT1 : (c + 1) * LT * SLOT1] = slots.reshape(LT * SLOT1, PAIRS, TILE)

    for c in range(COLS, DEVS // LT):
        put(c, jnp.zeros((TILE, TILE), F32))
    out.send(PIECES * SLOT1, DEVS * SLOT1)
    rows = jnp.concatenate([text_in()[...], cot_in()[...]], axis=0).reshape(TILE, D)
    pieces = mm(perm, rows)
    for c in range(COLS):
        put(c, pieces[:, c * TILE : (c + 1) * TILE])
        out.send(c * LT * SLOT1, (c + 1) * LT * SLOT1)


def column_to_row(rows, *lanes):
    pick = jnp.zeros((8, TILE), BF)
    for k, lane in enumerate(lanes):
        here = jnp.logical_and(iota((8, TILE), 0) == k, iota((8, TILE), 1) == lane)
        pick = pick + one_hot(here)
    return mm(pick, rows, NT)


def rank_pairs(ids):
    total = DEVS * PAIRS
    owner_col = ids[:, 0:1]
    owner_row = column_to_row(ids.astype(BF), 0)[0:1]
    step = 128
    ranks = []
    for b in range(total // step):
        earlier = iota((step, total), 1) < iota((step, total), 0) + b * step
        same = owner_col[b * step : (b + 1) * step] == owner_row
        ranks.append(
            jnp.sum(jnp.where(jnp.logical_and(same, earlier), 1.0, 0.0), axis=1, keepdims=True)
        )
    rank_col = jnp.concatenate(ranks, axis=0)
    with_rank = jnp.where(iota((total, TILE), 1) == 4, rank_col, ids).astype(BF)
    flat = column_to_row(with_rank, 0, 1, 4)
    return with_rank, flat[0:1] * PUSH + flat[2:3], flat[1:2]


def tile_rows(ref, k):
    tiles = ref[...].reshape(DEVS, SLOT1, PAIRS, TILE)[:, k]
    return tiles.astype(F32).reshape(DEVS * PAIRS, TILE)


def pick_kernel(got_in, out, ids_out, pair_tab):
    total = DEVS * PAIRS
    got = got_in()
    ids = tile_rows(got, 0)
    pair_tab[:, :TILE] = tile_rows(got, 1).astype(BF)
    pair_tab[:, TILE:] = tile_rows(got, 2).astype(BF)
    target_col = ids[:, 2:3] * PAIRS + ids[:, 3:4]
    with_rank, key_row, _ = rank_pairs(ids)
    ids_out.ref[...] = with_rank
    ids_out.send()
    slot_col = iota((DEVS * PUSH, 1), 0).astype(F32)
    pair_row = iota((1, total), 1).astype(F32)
    devs = 32
    for b in range(DEVS // devs):
        slots = slice(b * devs * PUSH, (b + 1) * devs * PUSH)
        pairs = slice(b * devs * PAIRS, (b + 1) * devs * PAIRS)
        pushed = mm(one_hot(slot_col[slots] == key_row), pair_tab[...])
        pulled = mm(one_hot(target_col[pairs] == pair_row), pair_tab[:, :TILE])
        tiles = jnp.concatenate(
            [
                pushed[:, :TILE].reshape(devs, 2, PAIRS, TILE),
                pushed[:, TILE:].reshape(devs, 2, PAIRS, TILE),
                pulled.reshape(devs, 1, PAIRS, TILE),
            ],
            axis=1,
        ).astype(BF)
        out.ref[b * devs * 5 : (b + 1) * devs * 5] = tiles.reshape(devs * 5, PAIRS, TILE)
        out.send(b * devs * 5, (b + 1) * devs * 5)


def sum_kernel(ids_in, got_in, out):
    total = DEVS * PAIRS
    ids_ref = ids_in()
    ids = ids_ref[...].astype(F32)
    key_col = ids[:, 0:1] * PUSH + ids[:, 4:5]
    flat = column_to_row(ids_ref[...], 2, 3)
    target_row = flat[0:1] * PAIRS + flat[1:2]
    pair_col = iota((total, 1), 0).astype(F32)
    slot_row = iota((1, DEVS * PUSH), 1).astype(F32)
    got = got_in()[...].astype(F32).reshape(DEVS, PUSH + PAIRS, TILE)
    push = got[:, :PUSH].reshape(DEVS * PUSH, TILE).astype(BF)
    pull = got[:, PUSH:].reshape(total, TILE).astype(BF)
    devs = 32
    for b in range(DEVS // devs):
        block = slice(b * devs * PAIRS, (b + 1) * devs * PAIRS)
        both = mm(one_hot(key_col[block] == slot_row), push)
        both += mm(one_hot(pair_col[block] == target_row), pull)
        out.ref[b * devs : (b + 1) * devs] = both.reshape(devs, PAIRS, TILE).astype(BF)
        out.send(b * devs, (b + 1) * devs)


def join_kernel(own_in, got_in, out):
    parts = []
    got_ref = got_in()
    for c in range(COLS):
        got = got_ref[c * LT : (c + 1) * LT].astype(F32)
        parts.append(got.reshape(LT * PAIRS, TILE).astype(BF))
    pieces = jnp.concatenate(parts, axis=1)
    out_row = iota((PAIRS * LT, LT * PAIRS), 0)
    in_row = iota((PAIRS * LT, LT * PAIRS), 1)
    perm = one_hot(in_row == (out_row & 15) * PAIRS + (out_row >> 4))
    total = own_in()[...] + mm(perm, pieces)
    out.ref[...] = total.astype(BF).reshape(PAIRS, LT, D)
    out.send()


def head_mask(scale=1.0):
    same = (iota((GR, GW), 0) >> 4) == (iota((GR, GW), 1) >> 6)
    return jnp.where(same, scale, 0.0).astype(BF)


def spread(rows, mask):
    return jnp.concatenate([rows] * GROUP, axis=0) * mask


def fold(full):
    head = iota((LT, GW), 1) >> 6
    out = full[0:LT]
    for h in range(1, GROUP):
        out = jnp.where(head == h, full[h * LT : (h + 1) * LT], out)
    return out


def parts_of(items, targets):
    for i, target in zip(items, targets):
        at = slice(i * LT, (i + 1) * LT)
        for g in range(GROUPS):
            yield i, target, at, slice(g * GW, (g + 1) * GW), slice(g * GR, (g + 1) * GR)


def attend(items, targets, keys_t, values, query, weights, probs, context):
    mask = head_mask(INV_ROOT)
    lane = iota((GR, LIR), 1)
    work = list(parts_of(items, targets))
    scores = []
    for i, target, at, cols, rows in work:
        s = mm(spread(query[at, cols], mask), keys_t[target, cols, :])
        scores.append(jnp.where(lane < LI, s, -1e30))
    halves = []
    for (i, target, at, cols, rows), s in zip(work, scores):
        w = jnp.exp(s - jnp.max(s, axis=1, keepdims=True))
        w = w * (1.0 / jnp.sum(w, axis=1, keepdims=True))
        half = w.astype(BF)
        weights[i, rows, :] = w
        probs[i, rows, :] = half
        halves.append(half)
    for (i, target, at, cols, rows), half in zip(work, halves):
        context[at, cols] = fold(mm(half, values[target, :, cols])).astype(BF)


def attend_back(items, targets, keys, values_t, d_context, weights, d_scores, d_query):
    mask = head_mask(INV_ROOT)
    work = list(parts_of(items, targets))
    d_probs = []
    for i, target, at, cols, rows in work:
        d_probs.append(mm(spread(d_context[at, cols], mask), values_t[target, cols, :]))
    halves = []
    for (i, target, at, cols, rows), dp in zip(work, d_probs):
        w = weights[i, rows, :]
        ds = w * (dp - jnp.sum(w * dp, axis=1, keepdims=True))
        ds = ds.astype(BF)
        d_scores[i, rows, :] = ds
        halves.append(ds)
    for (i, target, at, cols, rows), ds in zip(work, halves):
        d_query[at, cols] = fold(mm(ds, keys[target, :, cols])).astype(BF)


def norm_back(summed, cot, gain):
    centred = summed - jnp.mean(summed, axis=1, keepdims=True)
    inv_sigma = lax.rsqrt(jnp.mean(centred * centred, axis=1, keepdims=True) + NORM_EPS)
    normed = centred * inv_sigma
    gz = cot * gain
    return inv_sigma * (
        gz
        - jnp.mean(gz, axis=1, keepdims=True)
        - normed * jnp.mean(gz * normed, axis=1, keepdims=True)
    )


def project_kernel(
    image_in, wk_in, wv_in, keys_o, values_o, keys_t_o, values_t_o, wk_t_o, wv_t_o, padded
):
    image = image_in()
    padded[...] = jnp.zeros_like(padded)
    for t in range(PAIRS):
        padded[t * LIR : t * LIR + LI] = image[t]
    for w_in, plain, turned, w_t in (
        (wk_in, keys_o, keys_t_o, wk_t_o),
        (wv_in, values_o, values_t_o, wv_t_o),
    ):
        w = w_in()
        w_t.ref[...] = w[...].T
        w_t.send()
        for g in range(GROUPS):
            cols = slice(g * GW, (g + 1) * GW)
            made = mm(padded[...], w[:, cols]).astype(BF)
            for t in range(PAIRS):
                rows = made[t * LIR : (t + 1) * LIR]
                plain.ref[t, :, cols] = rows
                turned.ref[t, cols, :] = rows.T
        plain.send()
        turned.send()


def own_kernel(
    text_in, wq_in, keys_t_in, values_in, wo_in, gain_in, cot_in, values_t_in, keys_in,
    me_in, got_in,
    grad_o, d_scores, probs, query, d_context, meta_o, feats_o,
    weights, context, d_query,
):
    texts = text_in()[...].reshape(PAIRS * LT, D)
    query.ref[...] = mm(texts, wq_in()[...]).astype(BF)
    query.send()
    every = list(range(PAIRS))
    attend(every, every, keys_t_in(), values_in(), query.ref, weights, probs.ref, context)
    probs.send()
    wo = wo_in()[...]
    summed = mm(context[...], wo) + texts.astype(F32)
    cots = cot_in()[...].reshape(PAIRS * LT, D).astype(F32)
    d_summed = norm_back(summed, cots, gain_in()[...].reshape(1, D))
    d_context.ref[...] = mm(d_summed.astype(BF), wo.T).astype(BF)
    d_context.send()
    attend_back(
        every, every, keys_in(), values_t_in(), d_context.ref, weights, d_scores.ref, d_query
    )
    d_scores.send()
    grad_o.ref[...] = d_summed + mm(d_query[...], wq_in()[...].T)
    grad_o.send()
    total = DEVS * PAIRS
    got = got_in()
    feats_o.ref[...] = tile_rows(got, 0).astype(BF)
    feats_o.send()
    _, key_row, local_row = rank_pairs(tile_rows(got, 0))
    mine = (iota((PUSH, total), 0) + PUSH * me_in()[0]).astype(F32) == key_row
    live = jnp.sum(jnp.where(mine, 1.0, 0.0), axis=1, keepdims=True)
    target = jnp.sum(jnp.where(mine, local_row, 0.0), axis=1, keepdims=True)
    meta = jnp.where(live > 0, target, -1.0).astype(jnp.int32)
    meta_o.ref[...] = jnp.broadcast_to(meta, (PUSH, TILE))
    meta_o.send()


def guest_kernel(
    got_in, meta_in, cot_in, wq_in, keys_t_in, values_in, wo_in, gain_in,
    values_t_in, keys_in,
    out, query, probs, d_context, d_scores,
    weights, context, d_query, texts, cots, d_summed_ref,
):
    count = PUSH + PAIRS
    tiles = count // PAIRS
    out.ref[PIECES * tiles :] = jnp.zeros(((DEVS - PIECES) * tiles, PAIRS, TILE), BF)
    out.send(PIECES * tiles, DEVS * tiles)
    out_row = iota((20 * LT, 20 * LT), 0)
    in_row = iota((20 * LT, 20 * LT), 1)
    perm = one_hot(in_row == (out_row & 15) * 20 + (out_row >> 4))
    got_ref = got_in()
    parts = []
    for c in range(COLS):
        got = got_ref[c * LT * 5 : (c + 1) * LT * 5].astype(F32)
        parts.append(got.reshape(LT * 20, TILE).astype(BF))
    pieces = jnp.concatenate(parts, axis=1)
    rows = mm(perm, pieces)
    push_rows = PUSH * LT
    texts[:push_rows] = rows[:push_rows].astype(BF)
    texts[push_rows:] = rows[2 * push_rows :].astype(BF)
    cots[:push_rows] = rows[push_rows : 2 * push_rows].astype(BF)
    cots[push_rows:] = cot_in()[...].reshape(PAIRS * LT, D)
    wq = wq_in()[...]
    query.ref[...] = mm(texts[...], wq).astype(BF)
    query.send()
    meta = meta_in()
    own = list(range(PAIRS))
    keys_t, values = keys_t_in(), values_in()

    items = list(range(count))
    targets = [jnp.maximum(meta[i, 0], 0) for i in range(PUSH)] + own
    attend(items, targets, keys_t, values, query.ref, weights, probs.ref, context)
    probs.send()
    wo = wo_in()[...]
    summed = mm(context[...], wo) + texts[...].astype(F32)
    d_summed = norm_back(summed, cots[...].astype(F32), gain_in()[...].reshape(1, D))
    d_summed_ref[...] = d_summed
    d_context.ref[...] = mm(d_summed.astype(BF), wo.T).astype(BF)
    d_context.send()
    keys, values_t = keys_in(), values_t_in()

    attend_back(items, targets, keys, values_t, d_context.ref, weights, d_scores.ref, d_query)
    d_scores.send()
    grads = (d_summed_ref[...] + mm(d_query[...], wq.T)).astype(BF)
    out_row = iota((LT * count, count * LT), 0)
    in_row = iota((LT * count, count * LT), 1)
    row = out_row // count
    perm = one_hot(in_row == (out_row - row * count) * LT + row)
    back = mm(perm, grads)
    for c in range(COLS):
        block = slice(c * LT * tiles, (c + 1) * LT * tiles)
        part = back[:, c * TILE : (c + 1) * TILE]
        out.ref[block] = part.reshape(LT * tiles, PAIRS, TILE).astype(BF)
        out.send(block.start, block.stop)


def image_kernel(
    own_ds_in, own_q_in, ds_in, q_in, own_p_in, own_dc_in, p_in, dc_in, meta_in, wk_t_in, wv_t_in,
    out, d_keys, d_values,
):
    mask = head_mask()
    meta = meta_in()
    targets = [meta[i, 0] for i in range(PUSH)]
    sides = (
        (d_keys, own_ds_in, own_q_in, ds_in, q_in),
        (d_values, own_p_in, own_dc_in, p_in, dc_in),
    )
    for total, own_left_in, own_right_in, left_in, right_in in sides:
        own_left, own_right, left, right = own_left_in(), own_right_in(), left_in(), right_in()
        for g in range(GROUPS):
            cols = slice(g * GW, (g + 1) * GW)
            rows = slice(g * GR, (g + 1) * GR)
            visitors = [
                spread(right[i * LT : (i + 1) * LT, cols], mask) for i in range(PUSH)
            ]
            zero = jnp.zeros((GR, GW), BF)
            placed = jnp.concatenate(
                [
                    jnp.concatenate(
                        [jnp.where(targets[i] == t, visitors[i], zero) for t in range(PAIRS)],
                        axis=1,
                    )
                    for i in range(PUSH)
                ],
                axis=0,
            )
            visits = mm(left[0:PUSH, rows, :].reshape(PUSH * GR, LIR), placed, TN)
            for t in range(PAIRS):
                at = slice(t * LT, (t + 1) * LT)
                pat = slice((PUSH + t) * LT, (PUSH + t + 1) * LT)
                total[t, :, cols] = (visits[:, t * GW : (t + 1) * GW] + mm(
                    jnp.concatenate([own_left[t, rows, :], left[PUSH + t, rows, :]], axis=0),
                    jnp.concatenate(
                        [spread(own_right[at, cols], mask), spread(right[pat, cols], mask)], axis=0
                    ),
                    TN,
                )).astype(BF)
    d_keys_half = d_keys[...].reshape(PAIRS * LIR, D)
    d_values_half = d_values[...].reshape(PAIRS * LIR, D)
    wk_t, wv_t = wk_t_in(), wv_t_in()
    for g in range(GROUPS):
        cols = slice(g * GW, (g + 1) * GW)
        rows = mm(d_keys_half, wk_t[:, cols]) + mm(d_values_half, wv_t[:, cols])
        for t in range(PAIRS):
            out.ref[t, :, cols] = rows[t * LIR : (t + 1) * LIR].astype(BF)[:LI]
        out.send_columns(cols)


def log_sums(table):
    peak = jnp.max(table, axis=0, keepdims=True)
    return peak + jnp.log(jnp.sum(jnp.exp(table - peak), axis=0, keepdims=True))


def contrast_kernel(*refs):
    *feats_in, tf_in, if_in, me_in, d_text_o, d_image_o = refs
    total = DEVS * PAIRS
    me = me_in()[0]
    parts = [o()[...] for o in feats_in]
    for bit in (1, 2, 4):
        here = (me & bit) == bit
        parts = [jnp.where(here, parts[k ^ bit], parts[k]) for k in range(8)]
    lower = iota((total, TILE), 1) < TILE // 2

    def join(kind):
        halves = []
        for h in range(2):
            left = parts[4 * h + kind].astype(F32)
            right = parts[4 * h + 2 + kind].astype(F32)
            halves.append(jnp.where(lower, pltpu.roll(left, TILE // 2, 1), right).astype(BF))
        return jnp.concatenate(halves, axis=1)

    texts, images = join(0), join(1)
    texts_t, images_t = texts.T, images.T
    row_lse = log_sums(mm(images, texts_t) * SIM_SCALE)
    col_lse = log_sums(mm(texts, images_t) * SIM_SCALE)
    own = iota((PAIRS, total), 0) + me * PAIRS == iota((PAIRS, total), 1)

    def side(rows_in, turned, plain, across_lse, o):
        similar = mm(rows_in()[...], turned) * SIM_SCALE
        peak = jnp.max(similar, axis=1, keepdims=True)
        own_lse = peak + jnp.log(jnp.sum(jnp.exp(similar - peak), axis=1, keepdims=True))
        d_similar = 0.5 * jnp.exp(similar - own_lse) + 0.5 * jnp.exp(similar - across_lse)
        d_similar = d_similar - jnp.where(own, 1.0, 0.0)
        high = d_similar.astype(BF)
        rest = d_similar - high.astype(F32)
        middle = rest.astype(BF)
        low = (rest - middle.astype(F32)).astype(BF)
        o.ref[...] = SIM_SCALE * (mm(high, plain) + (mm(middle, plain) + mm(low, plain)))
        o.send()

    side(tf_in, images_t, images, col_lse, d_text_o)
    side(if_in, texts_t, texts, row_lse, d_image_o)


class Loaded:
    def __init__(self, src, dst, sem):
        self.copy = pltpu.make_async_copy(src, dst, sem)
        self.buffer = dst
        self.started = self.waited = False

    def start(self):
        if not self.started:
            self.copy.start()
            self.started = True

    def __call__(self):
        self.start()
        if not self.waited:
            self.copy.wait()
            self.waited = True
        return self.buffer


class Direct:
    def __init__(self, ref):
        self.buffer = ref

    def __call__(self):
        return self.buffer


class Stored:
    def __init__(self, ref, dst, sems, first):
        self.ref, self.dst, self.sems, self.first = ref, dst, sems, first
        self.copies = []

    def send(self, begin=None, end=None):
        ref, dst = self.ref, self.dst
        if begin is not None:
            ref, dst = ref.at[begin:end], dst.at[begin:end]
        self.start(ref, dst)

    def send_columns(self, cols):
        self.start(self.ref.at[:, :, cols], self.dst.at[:, :, cols])

    def start(self, ref, dst):
        copy = pltpu.make_async_copy(ref, dst, self.sems.at[self.first + len(self.copies)])
        copy.start()
        self.copies.append(copy)


def call(kernel, outs, args, scratch=(), flops=0, name=None, scalars=(), direct=(), mib=56, late=()):
    shapes = [jax.ShapeDtypeStruct(s, d) for s, d in outs]
    n, m = len(args), len(outs)
    size = sum(a.size * a.dtype.itemsize for a in args)
    size += sum(math.prod(s.shape) * s.dtype.itemsize for s in shapes)
    loaded = [k for k in range(n) if k not in direct]

    def body(*refs):
        arrays, refs = refs[: n + m], refs[n + m :]
        buffers, refs = refs[: len(loaded) + m], refs[len(loaded) + m :]
        sems, rest = refs[0], refs[1:]
        operands = [Direct(array) for array in arrays[:n]]
        for slot, k in enumerate(loaded):
            operands[k] = Loaded(arrays[k], buffers[slot], sems.at[slot])
            if k not in late:
                operands[k].start()
        stores = [
            Stored(buffers[len(loaded) + k], arrays[n + k], sems, n + k * SEND_PARTS)
            for k in range(m)
        ]
        kernel(*operands, *stores, *rest)
        for operand in operands:
            operand()
        for store in stores:
            for copy in store.copies:
                copy.wait()

    buffers = [
        (pltpu.SMEM if k in scalars else pltpu.VMEM)(args[k].shape, args[k].dtype) for k in loaded
    ]
    buffers += [pltpu.VMEM(s.shape, s.dtype) for s in shapes]
    far = pl.BlockSpec(memory_space=pltpu.HBM)
    near = pl.BlockSpec(memory_space=pltpu.VMEM)
    return pl.pallas_call(
        body,
        out_shape=shapes,
        in_specs=[near if k in direct else far for k in range(n)],
        out_specs=[far] * m,
        scratch_shapes=buffers
        + [pltpu.SemaphoreType.DMA((n + m * SEND_PARTS,))]
        + list(scratch),
        compiler_params=pltpu.CompilerParams(vmem_limit_bytes=mib * MIB),
        cost_estimate=pl.CostEstimate(flops=flops, bytes_accessed=size, transcendentals=0),
        name=name,
    )(*args)


def exchange(x):
    return lax.all_to_all(x, "dp", split_axis=0, concat_axis=0, tiled=True)


def on_device(
    text_states, image_states, cot_positive, cot_neg_image, cot_neg_text,
    w_query, w_key, w_value, w_out, ln_gain, neg_image, neg_text, text_feat, image_feat,
):
    me = lax.axis_index("dp").astype(jnp.int32).reshape(1)
    count = PUSH + PAIRS
    (send,) = call(
        pack_kernel,
        [((DEVS * SLOT1, PAIRS, TILE), BF)],
        (neg_image, neg_text, text_feat, image_feat, text_states, cot_neg_image),
        name="pack",
        scalars=(0, 1),
    )
    got = exchange(send)
    image_rows = ((PAIRS, LIR, D), BF)
    image_cols = ((PAIRS, D, LIR), BF)
    square = ((D, D), BF)
    keys, values, keys_t, values_t, wk_t, wv_t = call(
        project_kernel,
        [image_rows, image_rows, image_cols, image_cols, square, square],
        (image_states, w_key, w_value),
        [pltpu.VMEM((PAIRS * LIR, D), BF)],
        flops=4 * PAIRS * LIR * D * D,
        name="project",
    )
    got, keys = lax.optimization_barrier((got, keys))
    send, ids = call(
        pick_kernel,
        [((DEVS * 5, PAIRS, TILE), BF), ((DEVS * PAIRS, TILE), BF)],
        (got,),
        [pltpu.VMEM((DEVS * PAIRS, 2 * TILE), BF)],
        name="pick",
        direct=(0,),
        mib=16,
    )
    send, keys = lax.optimization_barrier((send, keys))
    got_rows = exchange(send)
    own_grad, own_ds, own_p, own_q, own_dc, meta, feats = call(
        own_kernel,
        [
            ((PAIRS * LT, D), F32),
            ((PAIRS, H * LT, LIR), BF),
            ((PAIRS, H * LT, LIR), BF),
            ((PAIRS * LT, D), BF),
            ((PAIRS * LT, D), BF),
            ((PUSH, TILE), jnp.int32),
            ((DEVS * PAIRS, TILE), BF),
        ],
        (
            text_states, w_query, keys_t, values, w_out, ln_gain, cot_positive,
            values_t, keys, me, got,
        ),
        [
            pltpu.VMEM((PAIRS, H * LT, LIR), F32),
            pltpu.VMEM((PAIRS * LT, D), BF),
            pltpu.VMEM((PAIRS * LT, D), BF),
        ],
        flops=8 * PAIRS * LT * D * D * 4,
        name="own",
        scalars=(9,),
        mib=63,
    )
    swapped = [
        lax.ppermute(feats, "dp", [(i, i ^ far) for i in range(DEVS)]) for far in range(1, 8)
    ]
    got_rows, own_grad = lax.optimization_barrier((got_rows, own_grad))
    send, q, p, dc, ds = call(
        guest_kernel,
        [
            ((DEVS * count // PAIRS, PAIRS, TILE), BF),
            ((count * LT, D), BF),
            ((count, H * LT, LIR), BF),
            ((count * LT, D), BF),
            ((count, H * LT, LIR), BF),
        ],
        (
            got_rows, meta, cot_neg_text, w_query, keys_t, values, w_out, ln_gain,
            values_t, keys,
        ),
        [
            pltpu.VMEM((count, H * LT, LIR), F32),
            pltpu.VMEM((count * LT, D), BF),
            pltpu.VMEM((count * LT, D), BF),
            pltpu.VMEM((count * LT, D), BF),
            pltpu.VMEM((count * LT, D), BF),
            pltpu.VMEM((count * LT, D), F32),
        ],
        flops=8 * count * LT * D * D * 4,
        name="guest",
        scalars=(1,),
    )
    got_back = exchange(send)
    (d_image,) = call(
        image_kernel,
        [((PAIRS, LI, D), BF)],
        (own_ds, own_q, ds, q, own_p, own_dc, p, dc, meta, wk_t, wv_t),
        [
            pltpu.VMEM((PAIRS, LIR, D), BF),
            pltpu.VMEM((PAIRS, LIR, D), BF),
        ],
        flops=8 * PAIRS * LIR * D * D,
        name="image",
        scalars=(8,),
    )
    got_back, d_image = lax.optimization_barrier((got_back, d_image))
    (send,) = call(sum_kernel, [((DEVS, PAIRS, TILE), BF)], (ids, got_back), name="sum", direct=(1,), mib=16)
    send, *swapped = lax.optimization_barrier((send, *swapped))
    got_sum = exchange(send)
    d_text_feat, d_image_feat = call(
        contrast_kernel,
        [((PAIRS, E), F32), ((PAIRS, E), F32)],
        (feats, *swapped, text_feat, image_feat, me),
        flops=8 * 512 * 512 * 256,
        name="contrast",
        scalars=(10,),
    )
    got_sum, d_text_feat, d_image_feat = lax.optimization_barrier(
        (got_sum, d_text_feat, d_image_feat)
    )
    (d_text,) = call(join_kernel, [((PAIRS, LT, D), BF)], (own_grad, got_sum), name="join", direct=(1,), mib=16)
    return (d_text, d_image, d_text_feat, d_image_feat)


def solution(mesh):
    return jax.shard_map(
        on_device,
        mesh=mesh,
        in_specs=(
            P("dp", None, None),
            P("dp", None, None),
            P("dp", None, None),
            P("dp", None, None),
            P("dp", None, None),
            P(),
            P(),
            P(),
            P(),
            P(),
            P("dp"),
            P("dp"),
            P("dp", None),
            P("dp", None),
        ),
        out_specs=(P("dp", None, None), P("dp", None, None), P("dp", None), P("dp", None)),
        check_vma=False,
    )
```
